256 devices in a mesh: ma: 128 (over z, y, x), bl: 2 (over core).
Axes of the slice: x: 4, y: 4, z: 8, core: 2. Of those that a mesh axis runs over, the one named last changes fastest.
Arguments:
- vis: float32 [2, 4096, 2048], P(None, 'ma', 'bl'), may hold values from -6 to 6
- counts: int32 [2048], P('bl'), may hold values from 1 to 256
- m_order: int32 [512], replicated, may hold values from 0 to 511, as said below
- beam: bfloat16 [512, 2, 2048, 512], P('ma', None, 'bl'), may hold values from -0.125 to 0.125
- row_counts: int32 [128], replicated, may hold values from 1 to 8, 512 in all
Outputs:
- alm_grad: float32 [2, 128, 4, 1024], P(None, None, 'bl', 'ma')
The draws below stay inside these ranges and needn't reach their ends.
Inputs may be any that keep to these rules, and one draw needn't show every extreme that they name: `m_order`: slot values are distinct multiples of 1 minus one, plus 512 // 512; every such value in range appears once. `row_counts`: counts sum to 512; each is at least 1 and one of them is exactly 8.
All inputs are finite; a program needn't handle non-finite values.
Results may differ from the reference program's by a relative error of at most 0.0029.
Values sent between devices are 32-bit elements; how exact they have to be, the bound alone decides.
No kernel may reach another device: no remote copies, remote signals or barrier semaphores. Data moves between devices by JAX's collectives and lax.ppermute only.
A program may use at most 64 MiB of HBM per device.

```python
import math
import jax
import jax.numpy as jnp
import numpy as np
from jax import lax

BASE = 2048
L = 512
M_DEV = 4
NT = 4096
NM = 512
ROWCAP = 8
N_MA = 128


def draw_m_order(key, part):
    key = jax.random.fold_in(key, 11)
    stride = L // NM
    order = jax.random.permutation(key, NM).astype(jnp.int32)
    return order * stride + (stride - 1)


def touch_ends(drawn, stream_key, smallest, top_value):
    place = [jax.random.randint(jax.random.fold_in(stream_key, axis), (), 0, length) for axis, length in enumerate(drawn.shape)]
    main_axis = drawn.shape.index(max(drawn.shape))
    beside = place[:main_axis] + [(place[main_axis] + 1) % drawn.shape[main_axis]] + place[main_axis + 1:]
    return drawn.at[tuple(place)].set(smallest).at[tuple(beside)].set(top_value)


def levels(rng, shape, pieces, least, top_value):
    loudness, own = 1.0, jax.random.fold_in(rng, 6)
    for position, parts in pieces:
        steps = jnp.exp(jax.random.uniform(jax.random.fold_in(own, position), (parts,), jnp.float32, least / len(pieces), top_value / len(pieces)))
        loudness = loudness * jnp.repeat(steps, shape[position] // parts).reshape([-1 if axis == position else 1 for axis in range(len(shape))])
    return loudness


def split_up(count, total, bound, slope):
    portions = [(1 << 20) // math.isqrt(rank ** slope) + 1 for rank in range(2, count + 1)]
    spare, holding = total - bound - (count - 1), [1] * (count - 1)
    while spare > 0:
        movable = [i for i in range(count - 1) if holding[i] < bound]
        pool, left = sum([portions[i] for i in movable]), spare
        for i in movable:
            extra = min(bound - holding[i], max(1, left * portions[i] // pool), spare)
            holding[i] = holding[i] + extra
            spare = spare - extra
    return np.array([bound] + holding)


def uneven(key, amount, total, reach, slope):
    if amount == 2:
        one = jax.random.randint(key, (), max(1, total - reach), min(reach, total - 1) + 1)
        return jnp.stack([one, total - one])
    tallies = jnp.asarray(split_up(amount, total, reach, slope), jnp.int32)
    couples = (amount - 1) // 2
    giver, taker = tallies[1:1 + 2 * couples:2], tallies[2:2 + 2 * couples:2]
    slack = jnp.minimum(giver - 1, reach - taker)
    passed = jax.random.randint(jax.random.fold_in(key, 1), (couples,), 0, 1 << 20) % (slack + 1)
    tallies = tallies.at[1:1 + 2 * couples:2].set(giver - passed).at[2:2 + 2 * couples:2].set(taker + passed)
    return tallies[jax.random.permutation(jax.random.fold_in(key, 2), amount)]


def centred(rng, extent, deviation, bound, cuts=(), kind=jnp.bfloat16):
    factor_of = levels(rng, extent, cuts, -0.22, 0.18) if cuts else 1.0
    array = jax.random.normal(rng, extent, jnp.float32) * deviation * factor_of
    return jnp.minimum(jnp.maximum(array, -bound), bound).astype(kind)


def setup_inputs(seed: int = 0) -> dict:
    key_of = jax.random.split(jax.random.key(seed), 6)
    return {
        "vis": centred(key_of[0], (2, NT, BASE), 1.0, 6.0, ((1, 128), (2, 2)), jnp.float32),
        "counts": touch_ends(jax.random.randint(key_of[1], (BASE,), 1, 257), jax.random.fold_in(key_of[1], 1), 1, 256).astype(jnp.int32),
        "m_order": draw_m_order(jax.random.fold_in(key_of[5], 71), 0),
        "beam": centred(key_of[3], (NM, 2, BASE, L), BASE ** -0.5, 0.125, ((0, 128), (2, 2))),
        "row_counts": uneven(key_of[4], N_MA, L, ROWCAP, 2).astype(jnp.int32),
    }


def reference(vis, counts, m_order, beam, row_counts):
    times = jnp.arange(NT, dtype=jnp.int32)
    turns = m_order[:, None] * times[None, :] % NT
    phase = 2.0 * jnp.pi / NT * turns.astype(jnp.float32)
    norm = 1.0 / jnp.sqrt(jnp.float32(NT))
    cosine = jnp.cos(phase) * norm
    sine = jnp.sin(phase) * norm
    high = lax.Precision.HIGHEST
    modes_re = jnp.dot(cosine, vis[0], precision=high) + jnp.dot(sine, vis[1], precision=high)
    modes_im = jnp.dot(cosine, vis[1], precision=high) - jnp.dot(sine, vis[0], precision=high)
    scale = counts.astype(jnp.float32) / 256.0
    weight_re = (modes_re * scale[None, :]).astype(jnp.bfloat16)
    weight_im = (modes_im * scale[None, :]).astype(jnp.bfloat16)
    ells = jnp.arange(L, dtype=jnp.int32)

    def one_mode(items):
        plane, wre, wim, mval = items
        real_part = plane[0].astype(jnp.float32)
        imag_part = plane[1].astype(jnp.float32)
        wre = wre.astype(jnp.float32)
        wim = wim.astype(jnp.float32)
        out_re = jnp.dot(wre, real_part) + jnp.dot(wim, imag_part)
        out_im = jnp.dot(wim, real_part) - jnp.dot(wre, imag_part)
        keep = ells >= mval
        return jnp.stack([jnp.where(keep, out_re, 0.0), jnp.where(keep, out_im, 0.0)])
    alm = lax.map(one_mode, (beam, weight_re, weight_im, m_order))
    starts = jnp.cumsum(row_counts) - row_counts
    rows = jnp.arange(N_MA * ROWCAP, dtype=jnp.int32)
    owner = rows // ROWCAP
    within = rows % ROWCAP
    ell_of_row = jnp.clip(starts[owner] + within, 0, L - 1)
    valid = within < row_counts[owner]
    picked = jnp.take(alm, ell_of_row, axis=2)
    picked = jnp.where(valid[None, None, :], picked, 0.0)
    result = jnp.transpose(picked, (1, 0, 2)).reshape(2, N_MA, M_DEV, N_MA * ROWCAP)
    return result
```

```python
import numpy as np
import jax
import jax.numpy as jnp
from jax import lax
from jax.experimental import pallas as pl
from jax.experimental.pallas import tpu as pltpu
from jax.sharding import Mesh
from jax.sharding import PartitionSpec as P

L = 512
TIMES = 4096
OUTER = 8
INNER = 16
SPAN = TIMES // OUTER
OWNERS = OUTER * INNER
SLOTS = 4
ROWCAP = 8
LANES = 128
HALF = 64

F32 = jnp.float32
BF16 = jnp.bfloat16
VMEM = pl.BlockSpec(memory_space=pltpu.VMEM)
SMEM = pl.BlockSpec(memory_space=pltpu.SMEM)
ANY = pl.BlockSpec(memory_space=pl.ANY)


def transform_tables():
    turns = np.outer(np.arange(L), np.arange(SPAN)) % TIMES
    phase = 2.0 * np.pi / TIMES * turns
    table = np.concatenate([np.cos(phase), np.sin(phase)], axis=1) / np.sqrt(TIMES)
    table = table.astype(np.float32)
    high = table.astype(BF16)
    low = (table - high.astype(np.float32)).astype(BF16)
    return high, low


def low_lanes(shape):
    return lax.broadcasted_iota(jnp.int32, shape, 1) < HALF


def quarter_turn(pair):
    turned = pltpu.roll(pair, HALF, 1)
    return jnp.where(low_lanes(pair.shape), turned, -turned)


def split(array):
    high = array.astype(BF16)
    return high, (array - high.astype(F32)).astype(BF16)


def pack_kernel(vis_ref, counts_ref, out_ref):
    low = low_lanes((vis_ref.shape[1], LANES))
    for j in range(vis_ref.shape[2] // LANES):
        lanes = slice(j * LANES, (j + 1) * LANES)
        scale = counts_ref[j : j + 1, :].astype(F32) * (1.0 / 256.0)
        re = vis_ref[0, :, lanes] * scale
        im = vis_ref[1, :, lanes] * scale
        out_ref[2 * j] = jnp.where(low, re, pltpu.roll(im, HALF, 1))
        out_ref[2 * j + 1] = jnp.where(low, pltpu.roll(re, HALF, 1), im)


def transform_kernel(order_ref, place_ref, x_ref, high_ref, low_ref, out_ref, modes_ref):
    x = x_ref[...]
    high, low = split(jnp.concatenate([x, quarter_turn(x)], axis=0))
    wide = jnp.dot(
        high_ref[...], jnp.concatenate([high, low], axis=1), preferred_element_type=F32
    )
    modes = wide[:, :LANES] + wide[:, LANES:]
    modes = modes + jnp.dot(low_ref[...], high, preferred_element_type=F32)
    eighths = lax.broadcasted_iota(jnp.int32, (8, LANES), 0) * place_ref[0] % 8
    angle = eighths.astype(F32) * (2.0 * np.pi / 8)
    cosine = jnp.cos(angle)[None]
    sine = jnp.sin(angle)[None]
    turned = quarter_turn(modes).reshape(L // 8, 8, LANES)
    modes = modes.reshape(L // 8, 8, LANES) * cosine + turned * sine
    modes_ref[...] = modes.reshape(L, LANES)

    def step(i, carry):
        for u in range(8):
            j = i * 8 + u
            out_ref[pl.ds(j, 1), :] = modes_ref[pl.ds(order_ref[j], 1), :]
        return carry

    lax.fori_loop(0, L // 8, step, 0, unroll=4)


def project_kernel(
    order_ref, place_ref, rows_ref, sums_ref, beam_ref, keep_ref, send_ref, held, sems
):
    def fetch(k):
        return pltpu.make_async_copy(beam_ref.at[k], held.at[k], sems.at[k])

    for k in range(SLOTS):
        fetch(k).start()

    counts = jnp.broadcast_to(rows_ref[...], (8, OWNERS))
    before = lax.broadcasted_iota(jnp.int32, (OWNERS, OWNERS), 0)
    before = before < lax.broadcasted_iota(jnp.int32, (OWNERS, OWNERS), 1)
    starts = jnp.dot(
        counts.astype(F32).astype(BF16),
        before.astype(F32).astype(BF16),
        preferred_element_type=F32,
    )
    starts = starts.astype(jnp.int32)[:1]
    counts = counts[:1]

    total = sums_ref[pl.ds(0, SLOTS * INNER), :]
    for z in range(1, OUTER):
        total = total + sums_ref[pl.ds(z * SLOTS * INNER, SLOTS * INNER), :]
    low = low_lanes((8, LANES))
    with_re, with_im = [], []
    for j in range(INNER // 2):
        tile = total[8 * j : 8 * j + 8]
        rolled = pltpu.roll(tile, HALF, 1)
        re = jnp.where(low, tile, pltpu.roll(rolled, 4, 0))[:4]
        im = jnp.where(low, rolled, pltpu.roll(tile, 4, 0))[:4]
        with_re.append(jnp.concatenate([re, im], axis=0))
        with_im.append(jnp.concatenate([im, -re], axis=0))
    weights = jnp.concatenate(with_re + with_im, axis=1).astype(BF16)

    ells = lax.broadcasted_iota(jnp.int32, (1, L), 1)
    rows = [None] * 8
    for k in range(SLOTS):
        fetch(k).wait()
        plane = held[k].reshape(2 * held.shape[2], L)
        product = jnp.dot(weights, plane, preferred_element_type=F32)
        keep = ells >= order_ref[place_ref[0] * SLOTS + k]
        at = k // 2 * 4 + k % 2
        rows[at] = jnp.where(keep, product[k : k + 1], 0.0)
        rows[at + 2] = jnp.where(keep, product[4 + k : 5 + k], 0.0)
    alm = jnp.concatenate(rows, axis=0)
    alm = jnp.concatenate(list(split(alm)), axis=0)

    first = place_ref[1] == 0
    at = lax.broadcasted_iota(jnp.int32, (L, OWNERS), 0)
    for pair in range(ROWCAP // 2):
        picks = []
        for q in (2 * pair, 2 * pair + 1):
            wanted = jnp.where(counts > q, starts + q, -1)
            picks.append(jnp.where(at == wanted, 1.0, 0.0).astype(BF16))
        picked = jnp.dot(alm, jnp.concatenate(picks, axis=1), preferred_element_type=F32)
        picked = picked[:8] + picked[8:]
        for i in range(2):
            block = picked[:, i * OWNERS : (i + 1) * OWNERS]
            rows_at = pl.ds(2 * pair + i, 4, stride=ROWCAP)
            keep_ref[rows_at, :] = jnp.where(first, block[:4], block[4:])
            send_ref[rows_at, :] = jnp.where(first, block[4:], block[:4])


def call(kernel, out_shape, in_specs, scratch_shapes=()):
    return pl.pallas_call(
        kernel,
        out_shape=out_shape,
        in_specs=in_specs,
        out_specs=jax.tree.map(lambda _: VMEM, out_shape),
        scratch_shapes=scratch_shapes,
        compiler_params=pltpu.CompilerParams(vmem_limit_bytes=32 * 1024 * 1024),
    )


def body(vis, counts, m_order, beam, row_counts):
    outer = lax.axis_index("outer")
    inner = lax.axis_index("inner")
    core = lax.axis_index("bl")
    share = vis.shape[1]
    bases = vis.shape[2]
    high, low = transform_tables()

    packed = call(
        pack_kernel, jax.ShapeDtypeStruct((INNER, share, LANES), F32), [VMEM, VMEM]
    )(vis, counts.reshape(bases // LANES, LANES))
    gathered = lax.all_to_all(packed, "inner", 0, 0, tiled=True)

    modes = call(
        transform_kernel,
        jax.ShapeDtypeStruct((L, LANES), F32),
        [SMEM, SMEM, VMEM, VMEM, VMEM],
        [pltpu.VMEM((L, LANES), F32)],
    )(
        m_order,
        outer.astype(jnp.int32).reshape(1),
        gathered.reshape(SPAN, LANES),
        jnp.asarray(high),
        jnp.asarray(low),
    )
    sums = lax.all_to_all(
        modes.reshape(OWNERS, SLOTS, LANES), ("outer", "inner"), 0, 0, tiled=True
    )

    place = jnp.stack([outer * INNER + inner, core]).astype(jnp.int32)
    half = jax.ShapeDtypeStruct((4 * ROWCAP, OWNERS), F32)
    keep, send = call(
        project_kernel,
        (half, half),
        [SMEM, SMEM, VMEM, VMEM, ANY],
        [pltpu.VMEM(beam.shape, BF16), pltpu.SemaphoreType.DMA((SLOTS,))],
    )(
        m_order,
        place,
        row_counts.reshape(1, OWNERS),
        sums.reshape(OWNERS * SLOTS, LANES),
        beam,
    )
    picked = keep + lax.ppermute(send, "bl", [(0, 1), (1, 0)])
    received = lax.all_to_all(picked.T, ("outer", "inner"), 0, 0, tiled=True)
    return received.T.reshape(2, 2, ROWCAP, OWNERS).transpose(0, 3, 1, 2)


def solution(mesh):
    mesh = Mesh(mesh.devices.reshape(OUTER, INNER, 2), ("outer", "inner", "bl"))
    ma = ("outer", "inner")
    placed = (P(None, ma, "bl"), P("bl"), P(), P(ma, None, "bl", None), P())
    return jax.shard_map(
        body, mesh=mesh, in_specs=placed, out_specs=P(None, None, "bl", ma), check_vma=False
    )
```

```python
import numpy as np
import jax
import jax.numpy as jnp
from jax import lax
from jax.experimental import pallas as pl
from jax.experimental.pallas import tpu as pltpu
from jax.sharding import Mesh
from jax.sharding import PartitionSpec as P

L = 512
TIMES = 4096
OUTER = 8
INNER = 16
SPAN = TIMES // OUTER
OWNERS = OUTER * INNER
SLOTS = 4
ROWCAP = 8
LANES = 128
HALF = 64
PARTS = 4
HELD = 6

F32 = jnp.float32
BF16 = jnp.bfloat16
I32 = jnp.int32
VMEM = pl.BlockSpec(memory_space=pltpu.VMEM)
SMEM = pl.BlockSpec(memory_space=pltpu.SMEM)
HBM = pl.BlockSpec(memory_space=pltpu.HBM)


def transform_tables():
    turns = np.outer(np.arange(L), np.arange(SPAN)) % TIMES
    phase = 2.0 * np.pi / TIMES * turns
    table = np.concatenate([np.cos(phase), np.sin(phase)], axis=1) / np.sqrt(TIMES)
    table = table.astype(np.float32)
    high = table.astype(BF16)
    low = (table - high.astype(np.float32)).astype(BF16)
    return high, low


def low_lanes(shape):
    return lax.broadcasted_iota(I32, shape, 1) < HALF


def quarter_turn(pair):
    turned = pltpu.roll(pair, HALF, 1)
    return jnp.where(low_lanes(pair.shape), turned, -turned)


def split(array):
    high = array.astype(BF16)
    return high, (array - high.astype(F32)).astype(BF16)


def ones_where(condition):
    return jnp.where(condition, 1.0, 0.0).astype(BF16)


def pack_kernel(vis_ref, counts_ref, out_ref, vis, counts, packed, in_sems, out_sems, sem):
    blocks = vis.shape[0]
    weigh = pltpu.make_async_copy(counts_ref, counts, sem)
    weigh.start()

    def fetch(j):
        lanes = pl.ds(j * LANES, LANES)
        return pltpu.make_async_copy(vis_ref.at[:, :, lanes], vis.at[j], in_sems.at[j])

    def store(j):
        two = pl.ds(2 * j, 2)
        return pltpu.make_async_copy(packed.at[two], out_ref.at[two], out_sems.at[j])

    for j in range(blocks):
        fetch(j).start()
    weigh.wait()
    low = low_lanes(vis.shape[2:])
    for j in range(blocks):
        fetch(j).wait()
        scale = counts[j : j + 1, :].astype(F32) * (1.0 / 256.0)
        re = vis[j, 0] * scale
        im = vis[j, 1] * scale
        packed[2 * j] = jnp.where(low, re, pltpu.roll(im, HALF, 1))
        packed[2 * j + 1] = jnp.where(low, pltpu.roll(re, HALF, 1), im)
        store(j).start()
    for j in range(blocks):
        store(j).wait()


def tables_kernel(
    outer_ref, high_hbm, low_hbm, order_hbm, high_ref, low_ref, pick_ref, turn_ref, order, sems
):
    copies = [
        pltpu.make_async_copy(order_hbm, order.at[pl.ds(0, L // LANES)], sems.at[0]),
        pltpu.make_async_copy(high_hbm, high_ref, sems.at[1]),
        pltpu.make_async_copy(low_hbm, low_ref, sems.at[2]),
    ]
    for copy in copies:
        copy.start()
    eighths = lax.broadcasted_iota(I32, (8, LANES), 0) * outer_ref[0] % 8
    angle = eighths.astype(F32) * (2.0 * np.pi / 8)
    turn_ref[0] = jnp.cos(angle)
    turn_ref[1] = jnp.sin(angle)
    copies[0].wait()
    columns = order[...].T
    modes = lax.broadcasted_iota(I32, (LANES, L), 1)
    for i in range(L // LANES):
        pick_ref[i * LANES : (i + 1) * LANES, :] = ones_where(modes == columns[:, i : i + 1])
    copies[1].wait()
    copies[2].wait()


def transform_kernel(
    x_ref, high_ref, low_ref, pick_ref, turn_ref, out_ref, token_ref, slots_ref, sem
):
    x = x_ref[...]
    high, low = split(jnp.concatenate([x, quarter_turn(x)], axis=0))
    wide = jnp.dot(
        high_ref[...], jnp.concatenate([high, low], axis=1), preferred_element_type=F32
    )
    modes = wide[:, :LANES] + wide[:, LANES:]
    modes = modes + jnp.dot(low_ref[...], high, preferred_element_type=F32)
    turned = quarter_turn(modes).reshape(L // 8, 8, LANES)
    modes = modes.reshape(L // 8, 8, LANES) * turn_ref[0][None] + turned * turn_ref[1][None]
    parts = jnp.concatenate(split(modes.reshape(L, LANES)), axis=1)
    slots = jnp.dot(pick_ref[...], parts, preferred_element_type=F32)
    slots_ref[...] = slots[:, :LANES] + slots[:, LANES:]
    token_ref[...] = jnp.zeros_like(token_ref)
    store = pltpu.make_async_copy(slots_ref, out_ref, sem)
    store.start()
    store.wait()


def held_kernel(
    place_ref,
    token_ref,
    order_hbm,
    rows_hbm,
    beam_hbm,
    held_ref,
    wanted_ref,
    keep_ref,
    order,
    rows,
    sems,
):
    rows_copy = pltpu.make_async_copy(rows_hbm, rows, sems.at[0])
    order_copy = pltpu.make_async_copy(order_hbm, order, sems.at[1])
    held_copy = pltpu.make_async_copy(beam_hbm.at[pl.ds(0, HELD)], held_ref, sems.at[2])
    rows_copy.start()
    order_copy.start()
    held_copy.start()

    order_copy.wait()
    ells = lax.broadcasted_iota(I32, (1, L), 1)
    for k in range(SLOTS):
        keep = jnp.where(ells >= order[place_ref[0] * SLOTS + k], 1.0, 0.0)
        at = k // 2 * 4 + k % 2
        keep_ref[at : at + 1, :] = keep
        keep_ref[at + 2 : at + 3, :] = keep

    rows_copy.wait()
    before = lax.broadcasted_iota(I32, (OWNERS, OWNERS), 0)
    before = ones_where(before < lax.broadcasted_iota(I32, (OWNERS, OWNERS), 1))
    counts = jnp.broadcast_to(rows[...], (ROWCAP, OWNERS))
    starts = jnp.dot(counts.astype(F32).astype(BF16), before, preferred_element_type=F32)
    within = lax.broadcasted_iota(I32, (ROWCAP, OWNERS), 0)
    wanted_ref[...] = jnp.where(within < counts, starts.astype(I32) + within, -1)
    held_copy.wait()


def project_kernel(
    core_ref,
    sums_ref,
    held_ref,
    wanted_ref,
    keep_ref,
    beam_hbm,
    own_ref,
    other_ref,
    beam,
    pick,
    sems,
):
    def fetch(i):
        return pltpu.make_async_copy(beam_hbm.at[i], beam.at[i - HELD], sems.at[i - HELD])

    for i in range(HELD, SLOTS * PARTS):
        fetch(i).start()

    at = lax.broadcasted_iota(I32, (L, OWNERS), 0)
    for q in range(ROWCAP):
        wanted = wanted_ref[q : q + 1, :]
        pick[:, q * OWNERS : (q + 1) * OWNERS] = ones_where(at == wanted)

    total = sums_ref[pl.ds(0, SLOTS * INNER), :]
    for z in range(1, OUTER):
        total = total + sums_ref[pl.ds(z * SLOTS * INNER, SLOTS * INNER), :]
    low = low_lanes((8, LANES))
    with_re, with_im = [], []
    for j in range(INNER // 2):
        tile = total[8 * j : 8 * j + 8]
        rolled = pltpu.roll(tile, HALF, 1)
        re = jnp.where(low, tile, pltpu.roll(rolled, 4, 0))[:4]
        im = jnp.where(low, rolled, pltpu.roll(tile, 4, 0))[:4]
        with_re.append(jnp.concatenate([re, im], axis=0))
        with_im.append(jnp.concatenate([im, -re], axis=0))
    weights = jnp.concatenate(with_re + with_im, axis=1).astype(BF16)
    depth = weights.shape[1] // PARTS

    def product(i):
        if i < HELD:
            block = held_ref[i]
        else:
            fetch(i).wait()
            block = beam[i - HELD]
        part = i % PARTS * depth
        return jnp.dot(weights[:, part : part + depth], block, preferred_element_type=F32)

    alm = [None] * 8
    for k in range(SLOTS):
        both = sum(product(k * PARTS + part) for part in range(PARTS))
        at = k // 2 * 4 + k % 2
        alm[at] = both[k : k + 1]
        alm[at + 2] = both[4 + k : 5 + k]
    alm = jnp.where(keep_ref[...] > 0.0, jnp.concatenate(alm, axis=0), 0.0)
    alm = jnp.concatenate(split(alm), axis=0)

    wide = jnp.dot(alm, pick[...], preferred_element_type=F32)
    wide = wide[:8] + wide[8:]
    first = core_ref[0] == 0
    for q in range(ROWCAP):
        block = wide[:, q * OWNERS : (q + 1) * OWNERS]
        rows_at = pl.ds(q, 4, stride=ROWCAP)
        own_ref[rows_at, :] = jnp.where(first, block[:4], block[4:])
        other_ref[rows_at, :] = jnp.where(first, block[4:], block[:4])


def call(kernel, out_shape, in_specs, scratch_shapes=(), scoped=8):
    return pl.pallas_call(
        kernel,
        out_shape=out_shape,
        in_specs=in_specs,
        out_specs=jax.tree.map(lambda a: pl.BlockSpec(memory_space=a.memory_space), out_shape),
        scratch_shapes=scratch_shapes,
        compiler_params=pltpu.CompilerParams(vmem_limit_bytes=scoped * 1024 * 1024),
    )


def in_hbm(array):
    return pltpu.with_memory_space_constraint(array, pltpu.HBM)


def in_vmem(array):
    return pltpu.with_memory_space_constraint(array, pltpu.VMEM)


def body(vis, counts, m_order, beam, row_counts):
    outer = lax.axis_index("outer")
    inner = lax.axis_index("inner")
    core = lax.axis_index("bl")
    share = vis.shape[1]
    blocks = vis.shape[2] // LANES
    high, low = transform_tables()
    dma = pltpu.SemaphoreType.DMA

    packed = call(
        pack_kernel,
        pltpu.HBM((INNER, share, LANES), F32),
        [HBM, HBM],
        [
            pltpu.VMEM((blocks, 2, share, LANES), F32),
            pltpu.VMEM((blocks, LANES), I32),
            pltpu.VMEM((INNER, share, LANES), F32),
            dma((blocks,)),
            dma((blocks,)),
            dma(()),
        ],
    )(in_hbm(vis), in_hbm(counts.reshape(blocks, LANES)))
    gathered = lax.all_to_all(packed, "inner", 0, 0, tiled=True)

    tables = call(
        tables_kernel,
        (
            pltpu.VMEM(high.shape, BF16),
            pltpu.VMEM(low.shape, BF16),
            pltpu.VMEM((L, L), BF16),
            pltpu.VMEM((2, 8, LANES), F32),
        ),
        [SMEM, HBM, HBM, HBM],
        [pltpu.VMEM((8, LANES), I32), dma((3,))],
    )(
        outer.astype(I32).reshape(1),
        in_hbm(jnp.asarray(high)),
        in_hbm(jnp.asarray(low)),
        in_hbm(m_order.reshape(L // LANES, LANES)),
    )
    modes, token = call(
        transform_kernel,
        (pltpu.HBM((L, LANES), F32), pltpu.VMEM((8, LANES), F32)),
        [VMEM] * 5,
        [pltpu.VMEM((L, LANES), F32), dma(())],
    )(gathered.reshape(SPAN, LANES), *map(in_vmem, tables))
    sums = lax.all_to_all(
        modes.reshape(OWNERS, SLOTS, LANES), ("outer", "inner"), 0, 0, tiled=True
    )

    beam = in_hbm(beam.reshape(SLOTS * PARTS, -1, L))
    held = call(
        held_kernel,
        (
            pltpu.VMEM((HELD, *beam.shape[1:]), BF16),
            pltpu.VMEM((ROWCAP, OWNERS), I32),
            pltpu.VMEM((8, L), F32),
        ),
        [SMEM, VMEM, HBM, HBM, HBM],
        [pltpu.SMEM((L,), I32), pltpu.VMEM((1, OWNERS), I32), dma((3,))],
    )(
        (outer * INNER + inner).astype(I32).reshape(1),
        token,
        in_hbm(m_order),
        in_hbm(row_counts.reshape(1, OWNERS)),
        beam,
    )
    half = pltpu.VMEM((4 * ROWCAP, OWNERS), F32)
    streamed = SLOTS * PARTS - HELD
    own, other = call(
        project_kernel,
        (half, half),
        [SMEM] + [VMEM] * 4 + [HBM],
        [
            pltpu.VMEM((streamed, *beam.shape[1:]), BF16),
            pltpu.VMEM((L, ROWCAP * OWNERS), BF16),
            dma((streamed,)),
        ],
        scoped=24,
    )(
        core.astype(I32).reshape(1),
        sums.reshape(OWNERS * SLOTS, LANES),
        *map(in_vmem, held),
        beam,
    )
    picked = own + lax.ppermute(other, "bl", [(0, 1), (1, 0)])
    received = lax.all_to_all(picked.T, ("outer", "inner"), 0, 0, tiled=True)
    return received.T.reshape(2, 2, ROWCAP, OWNERS).transpose(0, 3, 1, 2)


def solution(mesh):
    mesh = Mesh(mesh.devices.reshape(OUTER, INNER, 2), ("outer", "inner", "bl"))
    ma = ("outer", "inner")
    placed = (P(None, ma, "bl"), P("bl"), P(), P(ma, None, "bl", None), P())
    return jax.shard_map(
        body, mesh=mesh, in_specs=placed, out_specs=P(None, None, "bl", ma), check_vma=False
    )
```

```python
import numpy as np
import jax
import jax.numpy as jnp
from jax import lax
from jax.experimental import pallas as pl
from jax.experimental.pallas import tpu as pltpu
from jax.sharding import PartitionSpec as P

L = 512
TIMES = 4096
OUTER = 8
INNER = 16
SPAN = TIMES // OUTER
OWNERS = OUTER * INNER
SLOTS = 4
ROWCAP = 8
LANES = 128
HALF = 64
PARTS = 4
HELD = 6
FIRST_INNER = 10
FIRST_OUTER = 5
FIRST = FIRST_OUTER * INNER + FIRST_INNER
FIRST_LAST = FIRST

F32 = jnp.float32
BF16 = jnp.bfloat16
I32 = jnp.int32
VMEM = pl.BlockSpec(memory_space=pltpu.VMEM)
SMEM = pl.BlockSpec(memory_space=pltpu.SMEM)
HBM = pl.BlockSpec(memory_space=pltpu.HBM)


def transform_tables():
    times = np.arange(SPAN).reshape(INNER, -1)[np.arange(INNER) ^ FIRST_INNER]
    turns = np.outer(np.arange(L), times) % TIMES
    phase = 2.0 * np.pi / TIMES * turns
    table = np.concatenate([np.cos(phase), np.sin(phase)], axis=1) / np.sqrt(TIMES)
    table = table.astype(np.float32)
    high = table.astype(BF16)
    low = (table - high.astype(np.float32)).astype(BF16)
    return high, low


def low_lanes(shape):
    return lax.broadcasted_iota(I32, shape, 1) < HALF


def quarter_turn(pair):
    turned = pltpu.roll(pair, HALF, 1)
    return jnp.where(low_lanes(pair.shape), turned, -turned)


def split(array):
    high = array.astype(BF16)
    return high, (array - high.astype(F32)).astype(BF16)


def lane_xor(array, mask):
    lane = lax.broadcasted_iota(I32, array.shape, 1)
    for bit in range(7):
        step = 1 << bit
        if mask & step:
            up = pltpu.roll(array, LANES - step, 1)
            array = jnp.where(lane & step == 0, up, pltpu.roll(array, step, 1))
    return array


def ones_where(condition):
    return jnp.where(condition, 1.0, 0.0).astype(BF16)


def pack_kernel(vis_ref, counts_ref, out_ref, vis, counts, packed, in_sems, out_sems, sem):
    blocks = vis.shape[0]
    weigh = pltpu.make_async_copy(counts_ref, counts, sem)
    weigh.start()

    def fetch(j):
        lanes = pl.ds(j * LANES, LANES)
        return pltpu.make_async_copy(vis_ref.at[:, :, lanes], vis.at[j], in_sems.at[j])

    def store(j):
        two = pl.ds(2 * j, 2)
        return pltpu.make_async_copy(packed.at[two], out_ref.at[two], out_sems.at[j])

    for j in range(blocks):
        fetch(j).start()
    weigh.wait()
    low = low_lanes(vis.shape[2:])
    for j in range(blocks):
        fetch(j).wait()
        scale = counts[j : j + 1, :].astype(F32) * (1.0 / 256.0)
        re = vis[j, 0] * scale
        im = vis[j, 1] * scale
        packed[2 * j] = jnp.where(low, re, pltpu.roll(im, HALF, 1))
        packed[2 * j + 1] = jnp.where(low, pltpu.roll(re, HALF, 1), im)
        store(j).start()
    for j in range(blocks):
        store(j).wait()


def tables_kernel(
    outer_ref, high_hbm, low_hbm, order_hbm, high_ref, low_ref, pick_ref, turn_ref, order, sems
):
    copies = [
        pltpu.make_async_copy(order_hbm, order.at[pl.ds(0, L // LANES)], sems.at[0]),
        pltpu.make_async_copy(high_hbm, high_ref, sems.at[1]),
        pltpu.make_async_copy(low_hbm, low_ref, sems.at[2]),
    ]
    for copy in copies:
        copy.start()
    eighths = lax.broadcasted_iota(I32, (8, LANES), 0) * outer_ref[0] % 8
    angle = eighths.astype(F32) * (2.0 * np.pi / 8)
    turn_ref[0] = jnp.cos(angle)
    turn_ref[1] = jnp.sin(angle)
    copies[0].wait()
    columns = lane_xor(order[...], SLOTS * FIRST % LANES).T
    modes = lax.broadcasted_iota(I32, (LANES, L), 1)
    for i in range(L // LANES):
        block = i ^ SLOTS * FIRST // LANES
        pick_ref[i * LANES : (i + 1) * LANES, :] = ones_where(
            modes == columns[:, block : block + 1]
        )
    copies[1].wait()
    copies[2].wait()


def transform_kernel(
    x_ref, high_ref, low_ref, pick_ref, turn_ref, out_ref, token_ref, slots_ref, sem
):
    x = x_ref[...]
    high, low = split(jnp.concatenate([x, quarter_turn(x)], axis=0))
    wide = jnp.dot(
        high_ref[...], jnp.concatenate([high, low], axis=1), preferred_element_type=F32
    )
    modes = wide[:, :LANES] + wide[:, LANES:]
    modes = modes + jnp.dot(low_ref[...], high, preferred_element_type=F32)
    turned = quarter_turn(modes).reshape(L // 8, 8, LANES)
    modes = modes.reshape(L // 8, 8, LANES) * turn_ref[0][None] + turned * turn_ref[1][None]
    parts = jnp.concatenate(split(modes.reshape(L, LANES)), axis=1)
    slots = jnp.dot(pick_ref[...], parts, preferred_element_type=F32)
    slots_ref[...] = slots[:, :LANES] + slots[:, LANES:]
    token_ref[...] = jnp.zeros_like(token_ref)
    store = pltpu.make_async_copy(slots_ref, out_ref, sem)
    store.start()
    store.wait()


def held_kernel(
    place_ref,
    token_ref,
    order_hbm,
    rows_hbm,
    beam_hbm,
    held_ref,
    wanted_ref,
    keep_ref,
    order,
    rows,
    sems,
):
    rows_copy = pltpu.make_async_copy(rows_hbm, rows, sems.at[0])
    order_copy = pltpu.make_async_copy(order_hbm, order, sems.at[1])
    held_copy = pltpu.make_async_copy(beam_hbm.at[pl.ds(0, HELD)], held_ref, sems.at[2])
    rows_copy.start()
    order_copy.start()
    held_copy.start()

    order_copy.wait()
    ells = lax.broadcasted_iota(I32, (1, L), 1)
    for k in range(SLOTS):
        keep = jnp.where(ells >= order[place_ref[0] * SLOTS + k], 1.0, 0.0)
        at = k // 2 * 4 + k % 2
        keep_ref[at : at + 1, :] = keep
        keep_ref[at + 2 : at + 3, :] = keep

    rows_copy.wait()
    counts = jnp.broadcast_to(rows[...], (ROWCAP, OWNERS)).astype(F32).astype(BF16)
    other = lax.broadcasted_iota(I32, (OWNERS, OWNERS), 0)
    owner = lax.broadcasted_iota(I32, (OWNERS, OWNERS), 1) ^ FIRST_LAST
    starts = jnp.dot(counts, ones_where(other < owner), preferred_element_type=F32)
    counts = jnp.dot(counts, ones_where(other == owner), preferred_element_type=F32)
    counts = counts.astype(I32)
    within = lax.broadcasted_iota(I32, (ROWCAP, OWNERS), 0)
    wanted_ref[...] = jnp.where(within < counts, starts.astype(I32) + within, -1)
    held_copy.wait()


def project_kernel(
    core_ref,
    sums_ref,
    held_ref,
    wanted_ref,
    keep_ref,
    beam_hbm,
    own_ref,
    other_ref,
    beam,
    pick,
    sems,
):
    def fetch(i):
        return pltpu.make_async_copy(beam_hbm.at[i], beam.at[i - HELD], sems.at[i - HELD])

    for i in range(HELD, SLOTS * PARTS):
        fetch(i).start()

    at = lax.broadcasted_iota(I32, (L, OWNERS), 0)
    for q in range(ROWCAP):
        wanted = wanted_ref[q : q + 1, :]
        pick[:, q * OWNERS : (q + 1) * OWNERS] = ones_where(at == wanted)

    total = sums_ref[pl.ds(0, SLOTS * INNER), :]
    for z in range(1, OUTER):
        total = total + sums_ref[pl.ds(z * SLOTS * INNER, SLOTS * INNER), :]
    low = low_lanes((8, LANES))
    with_re, with_im = [], []
    for j in range(INNER // 2):
        tile = total[8 * j : 8 * j + 8]
        rolled = pltpu.roll(tile, HALF, 1)
        re = jnp.where(low, tile, pltpu.roll(rolled, 4, 0))[:4]
        im = jnp.where(low, rolled, pltpu.roll(tile, 4, 0))[:4]
        with_re.append(jnp.concatenate([re, im], axis=0))
        with_im.append(jnp.concatenate([im, -re], axis=0))
    weights = jnp.concatenate(with_re + with_im, axis=1).astype(BF16)
    depth = weights.shape[1] // PARTS

    def product(i):
        if i < HELD:
            block = held_ref[i]
        else:
            fetch(i).wait()
            block = beam[i - HELD]
        part = i % PARTS * depth
        return jnp.dot(weights[:, part : part + depth], block, preferred_element_type=F32)

    alm = [None] * 8
    for k in range(SLOTS):
        both = sum(product(k * PARTS + part) for part in range(PARTS))
        at = k // 2 * 4 + k % 2
        alm[at] = both[k : k + 1]
        alm[at + 2] = both[4 + k : 5 + k]
    alm = jnp.where(keep_ref[...] > 0.0, jnp.concatenate(alm, axis=0), 0.0)
    alm = jnp.concatenate(split(alm), axis=0)

    wide = jnp.dot(alm, pick[...], preferred_element_type=F32)
    wide = wide[:8] + wide[8:]
    first = core_ref[0] == 0
    for q in range(ROWCAP):
        block = wide[:, q * OWNERS : (q + 1) * OWNERS]
        rows_at = pl.ds(q, 4, stride=ROWCAP)
        own_ref[rows_at, :] = jnp.where(first, block[:4], block[4:])
        other_ref[rows_at, :] = jnp.where(first, block[4:], block[:4])


def finish_kernel(parts_ref, out_ref):
    out_ref[...] = lane_xor(parts_ref[...].T, FIRST_LAST)


def exchange(array, first, size):
    groups = [
        [base + (rank ^ first) for rank in range(size)] for base in range(0, OWNERS, size)
    ]
    return lax.all_to_all(array, "ma", 0, 0, axis_index_groups=groups, tiled=True)


def call(kernel, out_shape, in_specs, scratch_shapes=(), scoped=8):
    return pl.pallas_call(
        kernel,
        out_shape=out_shape,
        in_specs=in_specs,
        out_specs=jax.tree.map(
            lambda a: pl.BlockSpec(memory_space=getattr(a, "memory_space", pltpu.VMEM)), out_shape
        ),
        scratch_shapes=scratch_shapes,
        compiler_params=pltpu.CompilerParams(vmem_limit_bytes=scoped * 1024 * 1024),
    )


def in_hbm(array):
    return pltpu.with_memory_space_constraint(array, pltpu.HBM)


def in_vmem(array):
    return pltpu.with_memory_space_constraint(array, pltpu.VMEM)


def body(vis, counts, m_order, beam, row_counts):
    place = lax.axis_index("ma")
    core = lax.axis_index("bl")
    share = vis.shape[1]
    blocks = vis.shape[2] // LANES
    high, low = transform_tables()
    dma = pltpu.SemaphoreType.DMA

    packed = call(
        pack_kernel,
        pltpu.HBM((INNER, share, LANES), F32),
        [HBM, HBM],
        [
            pltpu.VMEM((blocks, 2, share, LANES), F32),
            pltpu.VMEM((blocks, LANES), I32),
            pltpu.VMEM((INNER, share, LANES), F32),
            dma((blocks,)),
            dma((blocks,)),
            dma(()),
        ],
    )(in_hbm(vis), in_hbm(counts.reshape(blocks, LANES)))
    gathered = exchange(packed, FIRST_INNER, INNER)

    tables = call(
        tables_kernel,
        (
            pltpu.VMEM(high.shape, BF16),
            pltpu.VMEM(low.shape, BF16),
            pltpu.VMEM((L, L), BF16),
            pltpu.VMEM((2, 8, LANES), F32),
        ),
        [SMEM, HBM, HBM, HBM],
        [pltpu.VMEM((8, LANES), I32), dma((3,))],
    )(
        (place // INNER).astype(I32).reshape(1),
        in_hbm(jnp.asarray(high)),
        in_hbm(jnp.asarray(low)),
        in_hbm(m_order.reshape(L // LANES, LANES)),
    )
    modes, token = call(
        transform_kernel,
        (pltpu.HBM((L, LANES), F32), pltpu.VMEM((8, LANES), F32)),
        [VMEM] * 5,
        [pltpu.VMEM((L, LANES), F32), dma(())],
    )(gathered.reshape(SPAN, LANES), *map(in_vmem, tables))
    sums = exchange(modes.reshape(OWNERS, SLOTS, LANES), FIRST, OWNERS)

    beam = in_hbm(beam.reshape(SLOTS * PARTS, -1, L))
    held = call(
        held_kernel,
        (
            pltpu.VMEM((HELD, *beam.shape[1:]), BF16),
            pltpu.VMEM((ROWCAP, OWNERS), I32),
            pltpu.VMEM((8, L), F32),
        ),
        [SMEM, VMEM, HBM, HBM, HBM],
        [pltpu.SMEM((L,), I32), pltpu.VMEM((1, OWNERS), I32), dma((3,))],
    )(
        place.astype(I32).reshape(1),
        token,
        in_hbm(m_order),
        in_hbm(row_counts.reshape(1, OWNERS)),
        beam,
    )
    half = pltpu.VMEM((4 * ROWCAP, OWNERS), F32)
    streamed = SLOTS * PARTS - HELD
    own, other = call(
        project_kernel,
        (half, half),
        [SMEM] + [VMEM] * 4 + [HBM],
        [
            pltpu.VMEM((streamed, *beam.shape[1:]), BF16),
            pltpu.VMEM((L, ROWCAP * OWNERS), BF16),
            dma((streamed,)),
        ],
        scoped=24,
    )(
        core.astype(I32).reshape(1),
        sums.reshape(OWNERS * SLOTS, LANES),
        *map(in_vmem, held),
        beam,
    )
    picked = own + lax.ppermute(other, "bl", [(0, 1), (1, 0)])
    received = exchange(picked.T, FIRST_LAST, OWNERS)
    out = call(finish_kernel, jax.ShapeDtypeStruct((4 * ROWCAP, OWNERS), F32), [VMEM])(received)
    return out.reshape(2, 2, ROWCAP, OWNERS).transpose(0, 3, 1, 2)


def solution(mesh):
    placed = (P(None, "ma", "bl"), P("bl"), P(), P("ma", None, "bl", None), P())
    return jax.shard_map(
        body, mesh=mesh, in_specs=placed, out_specs=P(None, None, "bl", "ma"), check_vma=False
    )
```

```python
import numpy as np
import jax
import jax.numpy as jnp
from jax import lax
from jax.experimental import pallas as pl
from jax.experimental.pallas import tpu as pltpu
from jax.sharding import PartitionSpec as P

L = 512
TIMES = 4096
OUTER = 8
INNER = 16
SPAN = TIMES // OUTER
OWNERS = OUTER * INNER
SLOTS = 4
ROWCAP = 8
LANES = 128
HALF = 64
PARTS = 4
HELD = 6
FIRST_INNER = 10
FIRST_OUTER = 5
FIRST = FIRST_OUTER * INNER + FIRST_INNER

F32 = jnp.float32
BF16 = jnp.bfloat16
I32 = jnp.int32
VMEM = pl.BlockSpec(memory_space=pltpu.VMEM)
SMEM = pl.BlockSpec(memory_space=pltpu.SMEM)
HBM = pl.BlockSpec(memory_space=pltpu.HBM)


def transform_table():
    times = np.arange(SPAN).reshape(INNER, -1)[np.arange(INNER) ^ FIRST_INNER]
    turns = np.outer(np.arange(L), times) % TIMES
    phase = 2.0 * np.pi / TIMES * turns
    table = np.concatenate([np.cos(phase), np.sin(phase)], axis=1) / np.sqrt(TIMES)
    return table.astype(np.float32)


def low_lanes(shape):
    return lax.broadcasted_iota(I32, shape, 1) < HALF


def quarter_turn(pair):
    turned = pltpu.roll(pair, HALF, 1)
    return jnp.where(low_lanes(pair.shape), turned, -turned)


def split(array):
    high = array.astype(BF16)
    return high, (array - high.astype(F32)).astype(BF16)


def lane_xor(array, mask):
    lane = lax.broadcasted_iota(I32, array.shape, 1)
    for bit in range(7):
        step = 1 << bit
        if mask & step:
            up = pltpu.roll(array, LANES - step, 1)
            array = jnp.where(lane & step == 0, up, pltpu.roll(array, step, 1))
    return array


def ones_where(condition):
    return jnp.where(condition, 1.0, 0.0).astype(BF16)


def pack_kernel(vis_ref, counts_ref, out_ref, vis, counts, packed, in_sems, out_sems):
    copies = [
        pltpu.make_async_copy(vis_ref, vis, in_sems.at[0]),
        pltpu.make_async_copy(counts_ref, counts, in_sems.at[1]),
    ]
    for copy in copies:
        copy.start()
    for copy in copies:
        copy.wait()

    def store(i):
        part = pl.ds(i * INNER // 2, INNER // 2)
        return pltpu.make_async_copy(packed.at[part], out_ref.at[part], out_sems.at[i])

    blocks = vis.shape[2] // LANES
    low = low_lanes((vis.shape[1], LANES))
    for j in range(blocks):
        lanes = slice(j * LANES, (j + 1) * LANES)
        scale = counts[j : j + 1, :].astype(F32) * (1.0 / 256.0)
        re = vis[0, :, lanes] * scale
        im = vis[1, :, lanes] * scale
        packed[2 * j] = jnp.where(low, re, pltpu.roll(im, HALF, 1))
        packed[2 * j + 1] = jnp.where(low, pltpu.roll(re, HALF, 1), im)
        if j % (blocks // 2) == blocks // 2 - 1:
            store(2 * j // blocks).start()
    for i in range(2):
        store(i).wait()


def tables_kernel(
    outer_ref, table_hbm, order_hbm, high_ref, low_ref, table, high, low, pick, order, sems
):
    order_copy = pltpu.make_async_copy(order_hbm, order.at[pl.ds(0, L // LANES)], sems.at[0])
    order_copy.start()

    def fetch(i):
        rows = pl.ds(i * LANES, LANES)
        return pltpu.make_async_copy(table_hbm.at[rows], table.at[rows], sems.at[i + 1])

    for i in range(L // LANES):
        fetch(i).start()
    eighths = lax.broadcasted_iota(I32, (8, LANES), 0) * outer_ref[0] % 8
    angle = eighths.astype(F32) * (2.0 * np.pi / 8)
    along = jnp.cos(angle)[None, :, :1]
    across = jnp.sin(angle)[None, :, :1]

    order_copy.wait()
    columns = lane_xor(order[...], SLOTS * FIRST % LANES).T
    modes = lax.broadcasted_iota(I32, (LANES, L), 1)
    for i in range(L // LANES):
        block = i ^ SLOTS * FIRST // LANES
        pick[i * LANES : (i + 1) * LANES, :] = ones_where(modes == columns[:, block : block + 1])

    for i in range(L // LANES):
        fetch(i).wait()
        rows = slice(i * LANES, (i + 1) * LANES)
        cosine = table[rows, :SPAN].reshape(LANES // 8, 8, SPAN)
        sine = table[rows, SPAN:].reshape(LANES // 8, 8, SPAN)
        turned = [cosine * along - sine * across, sine * along + cosine * across]
        turned = jnp.concatenate([part.reshape(LANES, SPAN) for part in turned], axis=1)
        high[rows, :], low[rows, :] = split(turned)
    for i in range(L // LANES):
        rows = slice(i * LANES, (i + 1) * LANES)
        for part, out_ref in ((high, high_ref), (low, low_ref)):
            picked = jnp.dot(pick[rows, :], part[...], preferred_element_type=F32)
            out_ref[rows, :] = picked.astype(BF16)


def transform_kernel(x_ref, high_ref, low_ref, out_ref, token_ref, slots_ref, sems):
    token_ref[...] = jnp.zeros_like(token_ref)
    x = x_ref[...]
    high, low = split(jnp.concatenate([x, quarter_turn(x)], axis=0))
    both = jnp.concatenate([high, low], axis=1)
    copies = []
    for i in range(2):
        rows = slice(i * L // 2, (i + 1) * L // 2)
        wide = jnp.dot(high_ref[rows, :], both, preferred_element_type=F32)
        slots = jnp.dot(low_ref[rows, :], high, preferred_element_type=F32)
        slots_ref[rows, :] = slots + wide[:, :LANES] + wide[:, LANES:]
        half = pl.ds(i * L // 2, L // 2)
        copies.append(pltpu.make_async_copy(slots_ref.at[half], out_ref.at[half], sems.at[i]))
        copies[i].start()
    for copy in copies:
        copy.wait()


def held_kernel(
    place_ref,
    token_ref,
    order_hbm,
    rows_hbm,
    beam_hbm,
    held_ref,
    wanted_ref,
    keep_ref,
    order,
    rows,
    sems,
):
    rows_copy = pltpu.make_async_copy(rows_hbm, rows, sems.at[0])
    order_copy = pltpu.make_async_copy(order_hbm, order, sems.at[1])
    held_copy = pltpu.make_async_copy(beam_hbm.at[pl.ds(0, HELD)], held_ref, sems.at[2])
    rows_copy.start()
    order_copy.start()
    held_copy.start()

    order_copy.wait()
    ells = lax.broadcasted_iota(I32, (1, L), 1)
    for k in range(SLOTS):
        keep = jnp.where(ells >= order[place_ref[0] * SLOTS + k], 1.0, 0.0)
        at = k // 2 * 4 + k % 2
        keep_ref[at : at + 1, :] = keep
        keep_ref[at + 2 : at + 3, :] = keep

    rows_copy.wait()
    counts = jnp.broadcast_to(rows[...], (ROWCAP, OWNERS)).astype(F32).astype(BF16)
    other = lax.broadcasted_iota(I32, (OWNERS, OWNERS), 0)
    owner = lax.broadcasted_iota(I32, (OWNERS, OWNERS), 1) ^ FIRST
    starts = jnp.dot(counts, ones_where(other < owner), preferred_element_type=F32)
    counts = jnp.dot(counts, ones_where(other == owner), preferred_element_type=F32)
    counts = counts.astype(I32)
    within = lax.broadcasted_iota(I32, (ROWCAP, OWNERS), 0)
    wanted_ref[...] = jnp.where(within < counts, starts.astype(I32) + within, -1)
    held_copy.wait()


def project_kernel(
    core_ref,
    sums_ref,
    held_ref,
    wanted_ref,
    keep_ref,
    beam_hbm,
    own_ref,
    other_ref,
    beam,
    pick,
    sems,
):
    def fetch(i):
        return pltpu.make_async_copy(beam_hbm.at[i], beam.at[i - HELD], sems.at[i - HELD])

    for i in range(HELD, SLOTS * PARTS):
        fetch(i).start()

    at = lax.broadcasted_iota(I32, (L, OWNERS), 0)
    for q in range(ROWCAP):
        wanted = wanted_ref[q : q + 1, :]
        pick[:, q * OWNERS : (q + 1) * OWNERS] = ones_where(at == wanted)

    total = sums_ref[pl.ds(0, SLOTS * INNER), :]
    for z in range(1, OUTER):
        total = total + sums_ref[pl.ds(z * SLOTS * INNER, SLOTS * INNER), :]
    low = low_lanes((8, LANES))
    with_re, with_im = [], []
    for j in range(INNER // 2):
        tile = total[8 * j : 8 * j + 8]
        rolled = pltpu.roll(tile, HALF, 1)
        re = jnp.where(low, tile, pltpu.roll(rolled, 4, 0))[:4]
        im = jnp.where(low, rolled, pltpu.roll(tile, 4, 0))[:4]
        with_re.append(jnp.concatenate([re, im], axis=0))
        with_im.append(jnp.concatenate([im, -re], axis=0))
    weights = jnp.concatenate(with_re + with_im, axis=1).astype(BF16)
    depth = weights.shape[1] // PARTS

    def product(i):
        if i < HELD:
            block = held_ref[i]
        else:
            fetch(i).wait()
            block = beam[i - HELD]
        part = i % PARTS * depth
        return jnp.dot(weights[:, part : part + depth], block, preferred_element_type=F32)

    alm = [None] * 8
    for k in range(SLOTS):
        both = sum(product(k * PARTS + part) for part in range(PARTS))
        at = k // 2 * 4 + k % 2
        alm[at] = both[k : k + 1]
        alm[at + 2] = both[4 + k : 5 + k]
    alm = jnp.where(keep_ref[...] > 0.0, jnp.concatenate(alm, axis=0), 0.0)
    alm = jnp.concatenate(split(alm), axis=0)

    wide = jnp.dot(alm, pick[...], preferred_element_type=F32)
    wide = wide[:8] + wide[8:]
    first = core_ref[0] == 0
    for q in range(ROWCAP):
        block = wide[:, q * OWNERS : (q + 1) * OWNERS]
        rows_at = pl.ds(q, 4, stride=ROWCAP)
        own_ref[rows_at, :] = jnp.where(first, block[:4], block[4:])
        other_ref[rows_at, :] = jnp.where(first, block[4:], block[:4])


def finish_kernel(parts_ref, out_ref):
    tiles = [parts_ref[(i ^ FIRST // 8) * 8 : (i ^ FIRST // 8) * 8 + 8, :] for i in range(OWNERS // 8)]
    out_ref[...] = lane_xor(jnp.concatenate(tiles, axis=0).T, FIRST % 8)


def exchange(array, first, size):
    groups = [
        [base + (rank ^ first) for rank in range(size)] for base in range(0, OWNERS, size)
    ]
    return lax.all_to_all(array, "ma", 0, 0, axis_index_groups=groups, tiled=True)


def call(kernel, out_shape, in_specs, scratch_shapes=(), scoped=8):
    return pl.pallas_call(
        kernel,
        out_shape=out_shape,
        in_specs=in_specs,
        out_specs=jax.tree.map(
            lambda a: pl.BlockSpec(memory_space=getattr(a, "memory_space", pltpu.VMEM)), out_shape
        ),
        scratch_shapes=scratch_shapes,
        compiler_params=pltpu.CompilerParams(vmem_limit_bytes=scoped * 1024 * 1024),
    )


def in_hbm(array):
    return pltpu.with_memory_space_constraint(array, pltpu.HBM)


def in_vmem(array):
    return pltpu.with_memory_space_constraint(array, pltpu.VMEM)


def body(vis, counts, m_order, beam, row_counts):
    place = lax.axis_index("ma")
    core = lax.axis_index("bl")
    share = vis.shape[1]
    blocks = vis.shape[2] // LANES
    table = transform_table()
    dma = pltpu.SemaphoreType.DMA

    packed = call(
        pack_kernel,
        pltpu.HBM((INNER, share, LANES), F32),
        [HBM, HBM],
        [
            pltpu.VMEM(vis.shape, F32),
            pltpu.VMEM((blocks, LANES), I32),
            pltpu.VMEM((INNER, share, LANES), F32),
            dma((2,)),
            dma((2,)),
        ],
    )(in_hbm(vis), in_hbm(counts.reshape(blocks, LANES)))
    gathered = exchange(packed, FIRST_INNER, INNER)

    tables = call(
        tables_kernel,
        (pltpu.VMEM(table.shape, BF16), pltpu.VMEM(table.shape, BF16)),
        [SMEM, HBM, HBM],
        [
            pltpu.VMEM(table.shape, F32),
            pltpu.VMEM(table.shape, BF16),
            pltpu.VMEM(table.shape, BF16),
            pltpu.VMEM((L, L), BF16),
            pltpu.VMEM((8, LANES), I32),
            dma((L // LANES + 1,)),
        ],
        scoped=16,
    )(
        (place // INNER).astype(I32).reshape(1),
        in_hbm(jnp.asarray(table)),
        in_hbm(m_order.reshape(L // LANES, LANES)),
    )
    modes, token = call(
        transform_kernel,
        (pltpu.HBM((L, LANES), F32), pltpu.VMEM((8, LANES), F32)),
        [VMEM] * 3,
        [pltpu.VMEM((L, LANES), F32), dma((2,))],
    )(gathered.reshape(SPAN, LANES), *map(in_vmem, tables))
    sums = exchange(modes.reshape(OWNERS, SLOTS, LANES), FIRST, OWNERS)

    beam = in_hbm(beam.reshape(SLOTS * PARTS, -1, L))
    held = call(
        held_kernel,
        (
            pltpu.VMEM((HELD, *beam.shape[1:]), BF16),
            pltpu.VMEM((ROWCAP, OWNERS), I32),
            pltpu.VMEM((8, L), F32),
        ),
        [SMEM, VMEM, HBM, HBM, HBM],
        [pltpu.SMEM((L,), I32), pltpu.VMEM((1, OWNERS), I32), dma((3,))],
    )(
        place.astype(I32).reshape(1),
        token,
        in_hbm(m_order),
        in_hbm(row_counts.reshape(1, OWNERS)),
        beam,
    )
    half = pltpu.VMEM((4 * ROWCAP, OWNERS), F32)
    streamed = SLOTS * PARTS - HELD
    own, other = call(
        project_kernel,
        (half, half),
        [SMEM] + [VMEM] * 4 + [HBM],
        [
            pltpu.VMEM((streamed, *beam.shape[1:]), BF16),
            pltpu.VMEM((L, ROWCAP * OWNERS), BF16),
            dma((streamed,)),
        ],
        scoped=24,
    )(
        core.astype(I32).reshape(1),
        sums.reshape(OWNERS * SLOTS, LANES),
        *map(in_vmem, held),
        beam,
    )
    picked = own + lax.ppermute(other, "bl", [(0, 1), (1, 0)])
    received = exchange(picked.T, FIRST, OWNERS)
    out = call(finish_kernel, jax.ShapeDtypeStruct((4 * ROWCAP, OWNERS), F32), [VMEM])(received)
    return out.reshape(2, 2, ROWCAP, OWNERS).transpose(0, 3, 1, 2)


def solution(mesh):
    placed = (P(None, "ma", "bl"), P("bl"), P(), P("ma", None, "bl", None), P())
    return jax.shard_map(
        body, mesh=mesh, in_specs=placed, out_specs=P(None, None, "bl", "ma"), check_vma=False
    )
```

```python
import numpy as np
import jax
import jax.numpy as jnp
from jax import lax
from jax.experimental import pallas as pl
from jax.experimental.pallas import tpu as pltpu
from jax.sharding import PartitionSpec as P

L = 512
TIMES = 4096
OUTER = 8
INNER = 16
SPAN = TIMES // OUTER
OWNERS = OUTER * INNER
SLOTS = 4
ROWCAP = 8
LANES = 128
HALF = 64
PARTS = 4
HELD = 2
STREAM = (HELD, 10, 14, SLOTS * PARTS)
FIRST_INNER = 10
FIRST_OUTER = 5
FIRST = FIRST_OUTER * INNER + FIRST_INNER

F32 = jnp.float32
BF16 = jnp.bfloat16
I32 = jnp.int32
VMEM = pl.BlockSpec(memory_space=pltpu.VMEM)
SMEM = pl.BlockSpec(memory_space=pltpu.SMEM)
HBM = pl.BlockSpec(memory_space=pltpu.HBM)


def transform_table():
    times = np.arange(SPAN).reshape(INNER, -1)[np.arange(INNER) ^ FIRST_INNER]
    turns = np.outer(np.arange(L), times) % TIMES
    phase = 2.0 * np.pi / TIMES * turns
    table = np.concatenate([np.cos(phase), np.sin(phase)], axis=1) / np.sqrt(TIMES)
    return table.astype(np.float32)


def low_lanes(shape):
    return lax.broadcasted_iota(I32, shape, 1) < HALF


def quarter_turn(pair):
    turned = pltpu.roll(pair, HALF, 1)
    return jnp.where(low_lanes(pair.shape), turned, -turned)


def split(array):
    high = array.astype(BF16)
    return high, (array - high.astype(F32)).astype(BF16)


def lane_xor(array, mask):
    lane = lax.broadcasted_iota(I32, array.shape, 1)
    for bit in range(7):
        step = 1 << bit
        if mask & step:
            up = pltpu.roll(array, LANES - step, 1)
            array = jnp.where(lane & step == 0, up, pltpu.roll(array, step, 1))
    return array


def ones_where(condition):
    return jnp.where(condition, 1.0, 0.0).astype(BF16)


def pack_kernel(vis_ref, counts_ref, out_ref, vis, counts, packed, in_sems, out_sems):
    copies = [
        pltpu.make_async_copy(vis_ref, vis, in_sems.at[0]),
        pltpu.make_async_copy(counts_ref, counts, in_sems.at[1]),
    ]
    for copy in copies:
        copy.start()
    for copy in copies:
        copy.wait()

    def store(i):
        part = pl.ds(i * INNER // 2, INNER // 2)
        return pltpu.make_async_copy(packed.at[part], out_ref.at[part], out_sems.at[i])

    blocks = vis.shape[2] // LANES
    low = low_lanes((vis.shape[1], LANES))
    for j in range(blocks):
        lanes = slice(j * LANES, (j + 1) * LANES)
        scale = counts[j : j + 1, :].astype(F32) * (1.0 / 256.0)
        re = vis[0, :, lanes] * scale
        im = vis[1, :, lanes] * scale
        packed[2 * j] = jnp.where(low, re, pltpu.roll(im, HALF, 1))
        packed[2 * j + 1] = jnp.where(low, pltpu.roll(re, HALF, 1), im)
        if j % (blocks // 2) == blocks // 2 - 1:
            store(2 * j // blocks).start()
    for i in range(2):
        store(i).wait()


def tables_kernel(
    place_ref,
    table_hbm,
    lanes_hbm,
    order_hbm,
    rows_hbm,
    beam_hbm,
    high_ref,
    low_ref,
    held_ref,
    wanted_ref,
    keep_ref,
    core_ref,
    table,
    high,
    low,
    pick,
    lanes,
    order,
    rows,
    sems,
):
    lanes_copy = pltpu.make_async_copy(lanes_hbm, lanes.at[pl.ds(0, L // LANES)], sems.at[0])
    order_copy = pltpu.make_async_copy(order_hbm, order, sems.at[1])
    rows_copy = pltpu.make_async_copy(rows_hbm, rows, sems.at[2])
    held_copy = pltpu.make_async_copy(beam_hbm.at[pl.ds(0, HELD)], held_ref, sems.at[3])
    lanes_copy.start()
    order_copy.start()
    rows_copy.start()

    def fetch(i):
        part = pl.ds(i * LANES, LANES)
        return pltpu.make_async_copy(table_hbm.at[part], table.at[part], sems.at[i + 4])

    for i in range(L // LANES):
        fetch(i).start()
    held_copy.start()
    eighths = lax.broadcasted_iota(I32, (8, LANES), 0) * (place_ref[0] // INNER) % 8
    angle = eighths.astype(F32) * (2.0 * np.pi / 8)
    along = jnp.cos(angle)[None, :, :1]
    across = jnp.sin(angle)[None, :, :1]

    lanes_copy.wait()
    columns = lane_xor(lanes[...], SLOTS * FIRST % LANES).T
    modes = lax.broadcasted_iota(I32, (LANES, L), 1)
    for i in range(L // LANES):
        block = i ^ SLOTS * FIRST // LANES
        pick[i * LANES : (i + 1) * LANES, :] = ones_where(modes == columns[:, block : block + 1])

    core_ref[...] = jnp.broadcast_to(place_ref[1], (8, LANES))
    order_copy.wait()
    ells = lax.broadcasted_iota(I32, (1, L), 1)
    for k in range(SLOTS):
        keep = jnp.where(ells >= order[place_ref[0] * SLOTS + k], 1.0, 0.0)
        at = k // 2 * 4 + k % 2
        keep_ref[at : at + 1, :] = keep
        keep_ref[at + 2 : at + 3, :] = keep

    rows_copy.wait()
    counts = jnp.broadcast_to(rows[...], (ROWCAP, OWNERS)).astype(F32).astype(BF16)
    other = lax.broadcasted_iota(I32, (OWNERS, OWNERS), 0)
    owner = lax.broadcasted_iota(I32, (OWNERS, OWNERS), 1) ^ FIRST
    starts = jnp.dot(counts, ones_where(other < owner), preferred_element_type=F32)
    counts = jnp.dot(counts, ones_where(other == owner), preferred_element_type=F32)
    counts = counts.astype(I32)
    within = lax.broadcasted_iota(I32, (ROWCAP, OWNERS), 0)
    wanted_ref[...] = jnp.where(within < counts, starts.astype(I32) + within, -1)

    for i in range(L // LANES):
        fetch(i).wait()
        part = slice(i * LANES, (i + 1) * LANES)
        cosine = table[part, :SPAN].reshape(LANES // 8, 8, SPAN)
        sine = table[part, SPAN:].reshape(LANES // 8, 8, SPAN)
        turned = [cosine * along - sine * across, sine * along + cosine * across]
        turned = jnp.concatenate([half.reshape(LANES, SPAN) for half in turned], axis=1)
        high[part, :], low[part, :] = split(turned)
    for i in range(L // LANES):
        part = slice(i * LANES, (i + 1) * LANES)
        for source, out_ref in ((high, high_ref), (low, low_ref)):
            picked = jnp.dot(pick[part, :], source[...], preferred_element_type=F32)
            out_ref[part, :] = picked.astype(BF16)
    held_copy.wait()


def transform_kernel(x_ref, high_ref, low_ref, out_ref):
    x = x_ref[...]
    high, low = split(jnp.concatenate([x, quarter_turn(x)], axis=0))
    both = jnp.concatenate([high, low], axis=1)
    wide = jnp.dot(high_ref[...], both, preferred_element_type=F32)
    slots = jnp.dot(low_ref[...], high, preferred_element_type=F32)
    out_ref[...] = slots + wide[:, :LANES] + wide[:, LANES:]


def project_kernel(
    sums_ref,
    held_ref,
    wanted_ref,
    keep_ref,
    core_ref,
    beam_hbm,
    own_ref,
    other_ref,
    beam,
    pick,
    sems,
):
    copies = {}
    for i, (begin, end) in enumerate(zip(STREAM, STREAM[1:])):
        source = beam_hbm.at[pl.ds(begin, end - begin)]
        target = beam.at[pl.ds(begin - HELD, end - begin)]
        copies[begin] = pltpu.make_async_copy(source, target, sems.at[i])
        copies[begin].start()

    at = lax.broadcasted_iota(I32, (L, OWNERS), 0)
    for q in range(ROWCAP):
        wanted = wanted_ref[q : q + 1, :]
        pick[:, q * OWNERS : (q + 1) * OWNERS] = ones_where(at == wanted)

    total = sums_ref[pl.ds(0, SLOTS * INNER), :]
    for z in range(1, OUTER):
        total = total + sums_ref[pl.ds(z * SLOTS * INNER, SLOTS * INNER), :]
    low = low_lanes((8, LANES))
    with_re, with_im = [], []
    for j in range(INNER // 2):
        tile = total[8 * j : 8 * j + 8]
        rolled = pltpu.roll(tile, HALF, 1)
        re = jnp.where(low, tile, pltpu.roll(rolled, 4, 0))[:4]
        im = jnp.where(low, rolled, pltpu.roll(tile, 4, 0))[:4]
        with_re.append(jnp.concatenate([re, im], axis=0))
        with_im.append(jnp.concatenate([im, -re], axis=0))
    weights = jnp.concatenate(with_re + with_im, axis=1).astype(BF16)
    depth = weights.shape[1] // PARTS

    def product(i):
        if i < HELD:
            block = held_ref[i]
        else:
            if i in copies:
                copies[i].wait()
            block = beam[i - HELD]
        part = i % PARTS * depth
        return jnp.dot(weights[:, part : part + depth], block, preferred_element_type=F32)

    alm = [None] * 8
    for k in range(SLOTS):
        both = sum(product(k * PARTS + part) for part in range(PARTS))
        at = k // 2 * 4 + k % 2
        alm[at] = both[k : k + 1]
        alm[at + 2] = both[4 + k : 5 + k]
    alm = jnp.where(keep_ref[...] > 0.0, jnp.concatenate(alm, axis=0), 0.0)
    alm = jnp.concatenate(split(alm), axis=0)

    wide = jnp.dot(alm, pick[...], preferred_element_type=F32)
    wide = wide[:8] + wide[8:]
    first = core_ref[:4] == 0
    for q in range(ROWCAP):
        block = wide[:, q * OWNERS : (q + 1) * OWNERS]
        rows_at = pl.ds(q, 4, stride=ROWCAP)
        own_ref[rows_at, :] = jnp.where(first, block[:4], block[4:])
        other_ref[rows_at, :] = jnp.where(first, block[4:], block[:4])


def finish_kernel(parts_ref, out_ref):
    starts = [8 * (i ^ FIRST // 8) for i in range(OWNERS // 8)]
    tiles = [parts_ref[start : start + 8, :] for start in starts]
    out_ref[...] = lane_xor(jnp.concatenate(tiles, axis=0).T, FIRST % 8)


def exchange(array, first, size):
    groups = [
        [base + (rank ^ first) for rank in range(size)] for base in range(0, OWNERS, size)
    ]
    return lax.all_to_all(array, "ma", 0, 0, axis_index_groups=groups, tiled=True)


def call(kernel, out_shape, in_specs, scratch_shapes=(), scoped=8):
    return pl.pallas_call(
        kernel,
        out_shape=out_shape,
        in_specs=in_specs,
        out_specs=jax.tree.map(
            lambda a: pl.BlockSpec(memory_space=getattr(a, "memory_space", pltpu.VMEM)), out_shape
        ),
        scratch_shapes=scratch_shapes,
        compiler_params=pltpu.CompilerParams(vmem_limit_bytes=scoped * 1024 * 1024),
    )


def in_hbm(array):
    return pltpu.with_memory_space_constraint(array, pltpu.HBM)


def in_vmem(array):
    return pltpu.with_memory_space_constraint(array, pltpu.VMEM)


def body(vis, counts, m_order, beam, row_counts):
    place = lax.axis_index("ma")
    share = vis.shape[1]
    blocks = vis.shape[2] // LANES
    table = transform_table()
    dma = pltpu.SemaphoreType.DMA

    packed = call(
        pack_kernel,
        pltpu.HBM((INNER, share, LANES), F32),
        [HBM, HBM],
        [
            pltpu.VMEM(vis.shape, F32),
            pltpu.VMEM((blocks, LANES), I32),
            pltpu.VMEM((INNER, share, LANES), F32),
            dma((2,)),
            dma((2,)),
        ],
    )(in_hbm(vis), in_hbm(counts.reshape(blocks, LANES)))
    gathered = exchange(packed, FIRST_INNER, INNER)

    beam = in_hbm(beam.reshape(SLOTS * PARTS, -1, L))
    high, low, *held = call(
        tables_kernel,
        (
            pltpu.VMEM(table.shape, BF16),
            pltpu.VMEM(table.shape, BF16),
            pltpu.VMEM((HELD, *beam.shape[1:]), BF16),
            pltpu.VMEM((ROWCAP, OWNERS), I32),
            pltpu.VMEM((8, L), F32),
            pltpu.VMEM((8, LANES), I32),
        ),
        [SMEM] + [HBM] * 5,
        [
            pltpu.VMEM(table.shape, F32),
            pltpu.VMEM(table.shape, BF16),
            pltpu.VMEM(table.shape, BF16),
            pltpu.VMEM((L, L), BF16),
            pltpu.VMEM((8, LANES), I32),
            pltpu.SMEM((L,), I32),
            pltpu.VMEM((1, OWNERS), I32),
            dma((L // LANES + 4,)),
        ],
        scoped=16,
    )(
        jnp.stack([place, lax.axis_index("bl")]).astype(I32),
        in_hbm(jnp.asarray(table)),
        in_hbm(m_order.reshape(L // LANES, LANES)),
        in_hbm(m_order),
        in_hbm(row_counts.reshape(1, OWNERS)),
        beam,
    )
    modes = call(transform_kernel, pltpu.VMEM((L, LANES), F32), [VMEM] * 3)(
        gathered.reshape(SPAN, LANES), in_vmem(high), in_vmem(low)
    )
    sums = exchange(modes.reshape(OWNERS, SLOTS, LANES), FIRST, OWNERS)

    half = pltpu.VMEM((4 * ROWCAP, OWNERS), F32)
    streamed = SLOTS * PARTS - HELD
    own, other = call(
        project_kernel,
        (half, half),
        [VMEM] * 5 + [HBM],
        [
            pltpu.VMEM((streamed, *beam.shape[1:]), BF16),
            pltpu.VMEM((L, ROWCAP * OWNERS), BF16),
            dma((len(STREAM) - 1,)),
        ],
        scoped=24,
    )(
        sums.reshape(OWNERS * SLOTS, LANES),
        *map(in_vmem, held),
        beam,
    )
    picked = own + lax.ppermute(other, "bl", [(0, 1), (1, 0)])
    received = exchange(picked.T, FIRST, OWNERS)
    out = call(finish_kernel, jax.ShapeDtypeStruct((4 * ROWCAP, OWNERS), F32), [VMEM])(received)
    return out.reshape(2, 2, ROWCAP, OWNERS).transpose(0, 3, 1, 2)


def solution(mesh):
    placed = (P(None, "ma", "bl"), P("bl"), P(), P("ma", None, "bl", None), P())
    return jax.shard_map(
        body, mesh=mesh, in_specs=placed, out_specs=P(None, None, "bl", "ma"), check_vma=False
    )
```

```python
import numpy as np
import jax
import jax.numpy as jnp
from jax import lax
from jax.experimental import pallas as pl
from jax.experimental.pallas import tpu as pltpu
from jax.sharding import PartitionSpec as P

L = 512
TIMES = 4096
OUTER = 8
INNER = 16
SPAN = TIMES // OUTER
OWNERS = OUTER * INNER
SLOTS = 4
ROWCAP = 8
LANES = 128
HALF = 64
PARTS = 4
HELD = 2
STREAM = (HELD, 10, 14, SLOTS * PARTS)
FIRST_INNER = 10
FIRST_OUTER = 5
FIRST = FIRST_OUTER * INNER + FIRST_INNER
FIRST_LAST = 74

F32 = jnp.float32
BF16 = jnp.bfloat16
I32 = jnp.int32
VMEM = pl.BlockSpec(memory_space=pltpu.VMEM)
SMEM = pl.BlockSpec(memory_space=pltpu.SMEM)
HBM = pl.BlockSpec(memory_space=pltpu.HBM)


def transform_table():
    times = np.arange(SPAN).reshape(INNER, -1)[np.arange(INNER) ^ FIRST_INNER]
    turns = np.outer(np.arange(L), times) % TIMES
    phase = 2.0 * np.pi / TIMES * turns
    table = np.concatenate([np.cos(phase), np.sin(phase)], axis=1) / np.sqrt(TIMES)
    return table.astype(np.float32)


def low_lanes(shape):
    return lax.broadcasted_iota(I32, shape, 1) < HALF


def quarter_turn(pair):
    turned = pltpu.roll(pair, HALF, 1)
    return jnp.where(low_lanes(pair.shape), turned, -turned)


def split(array):
    high = array.astype(BF16)
    return high, (array - high.astype(F32)).astype(BF16)


def lane_xor(array, mask):
    lane = lax.broadcasted_iota(I32, array.shape, 1)
    for bit in range(7):
        step = 1 << bit
        if mask & step:
            up = pltpu.roll(array, LANES - step, 1)
            array = jnp.where(lane & step == 0, up, pltpu.roll(array, step, 1))
    return array


def ones_where(condition):
    return jnp.where(condition, 1.0, 0.0).astype(BF16)


def pack_kernel(vis_ref, counts_ref, out_ref, vis, counts, packed, in_sems, out_sems):
    copies = [
        pltpu.make_async_copy(vis_ref, vis, in_sems.at[0]),
        pltpu.make_async_copy(counts_ref, counts, in_sems.at[1]),
    ]
    for copy in copies:
        copy.start()
    for copy in copies:
        copy.wait()

    def store(i):
        part = pl.ds(i * INNER // 2, INNER // 2)
        return pltpu.make_async_copy(packed.at[part], out_ref.at[part], out_sems.at[i])

    blocks = vis.shape[2] // LANES
    low = low_lanes((vis.shape[1], LANES))
    for j in range(blocks):
        lanes = slice(j * LANES, (j + 1) * LANES)
        scale = counts[j : j + 1, :].astype(F32) * (1.0 / 256.0)
        re = vis[0, :, lanes] * scale
        im = vis[1, :, lanes] * scale
        packed[2 * j] = jnp.where(low, re, pltpu.roll(im, HALF, 1))
        packed[2 * j + 1] = jnp.where(low, pltpu.roll(re, HALF, 1), im)
        if j % (blocks // 2) == blocks // 2 - 1:
            store(2 * j // blocks).start()
    for i in range(2):
        store(i).wait()


def tables_kernel(
    place_ref,
    table_hbm,
    lanes_hbm,
    order_hbm,
    rows_hbm,
    beam_hbm,
    high_ref,
    low_ref,
    held_ref,
    wanted_ref,
    keep_ref,
    core_ref,
    table,
    high,
    low,
    pick,
    lanes,
    order,
    rows,
    sems,
):
    lanes_copy = pltpu.make_async_copy(lanes_hbm, lanes.at[pl.ds(0, L // LANES)], sems.at[0])
    order_copy = pltpu.make_async_copy(order_hbm, order, sems.at[1])
    rows_copy = pltpu.make_async_copy(rows_hbm, rows, sems.at[2])
    held_copy = pltpu.make_async_copy(beam_hbm.at[pl.ds(0, HELD)], held_ref, sems.at[3])
    lanes_copy.start()
    order_copy.start()
    rows_copy.start()

    def fetch(i):
        part = pl.ds(i * LANES, LANES)
        return pltpu.make_async_copy(table_hbm.at[part], table.at[part], sems.at[i + 4])

    for i in range(L // LANES):
        fetch(i).start()
    held_copy.start()
    eighths = lax.broadcasted_iota(I32, (8, LANES), 0) * (place_ref[0] // INNER) % 8
    angle = eighths.astype(F32) * (2.0 * np.pi / 8)
    along = jnp.cos(angle)[None, :, :1]
    across = jnp.sin(angle)[None, :, :1]

    lanes_copy.wait()
    columns = lane_xor(lanes[...], SLOTS * FIRST % LANES).T
    modes = lax.broadcasted_iota(I32, (LANES, L), 1)
    for i in range(L // LANES):
        block = i ^ SLOTS * FIRST // LANES
        pick[i * LANES : (i + 1) * LANES, :] = ones_where(modes == columns[:, block : block + 1])

    core_ref[...] = jnp.broadcast_to(place_ref[1], (8, LANES))
    order_copy.wait()
    ells = lax.broadcasted_iota(I32, (1, L), 1)
    for k in range(SLOTS):
        keep = jnp.where(ells >= order[place_ref[0] * SLOTS + k], 1.0, 0.0)
        at = k // 2 * 4 + k % 2
        keep_ref[at : at + 1, :] = keep
        keep_ref[at + 2 : at + 3, :] = keep

    rows_copy.wait()
    counts = jnp.broadcast_to(rows[...], (ROWCAP, OWNERS)).astype(F32).astype(BF16)
    other = lax.broadcasted_iota(I32, (OWNERS, OWNERS), 0)
    owner = lax.broadcasted_iota(I32, (OWNERS, OWNERS), 1) ^ FIRST_LAST
    starts = jnp.dot(counts, ones_where(other < owner), preferred_element_type=F32)
    counts = jnp.dot(counts, ones_where(other == owner), preferred_element_type=F32)
    counts = counts.astype(I32)
    within = lax.broadcasted_iota(I32, (ROWCAP, OWNERS), 0)
    wanted_ref[...] = jnp.where(within < counts, starts.astype(I32) + within, -1)

    for i in range(L // LANES):
        fetch(i).wait()
        part = slice(i * LANES, (i + 1) * LANES)
        cosine = table[part, :SPAN].reshape(LANES // 8, 8, SPAN)
        sine = table[part, SPAN:].reshape(LANES // 8, 8, SPAN)
        turned = [cosine * along - sine * across, sine * along + cosine * across]
        turned = jnp.concatenate([half.reshape(LANES, SPAN) for half in turned], axis=1)
        high[part, :], low[part, :] = split(turned)
    for i in range(L // LANES):
        part = slice(i * LANES, (i + 1) * LANES)
        for source, out_ref in ((high, high_ref), (low, low_ref)):
            picked = jnp.dot(pick[part, :], source[...], preferred_element_type=F32)
            out_ref[part, :] = picked.astype(BF16)
    held_copy.wait()


def transform_kernel(x_ref, high_ref, low_ref, out_ref):
    x = x_ref[...]
    high, low = split(jnp.concatenate([x, quarter_turn(x)], axis=0))
    both = jnp.concatenate([high, low], axis=1)
    wide = jnp.dot(high_ref[...], both, preferred_element_type=F32)
    slots = jnp.dot(low_ref[...], high, preferred_element_type=F32)
    out_ref[...] = slots + wide[:, :LANES] + wide[:, LANES:]


def project_kernel(
    sums_ref,
    held_ref,
    wanted_ref,
    keep_ref,
    core_ref,
    beam_hbm,
    own_ref,
    other_ref,
    beam,
    pick,
    sems,
):
    copies = {}
    for i, (begin, end) in enumerate(zip(STREAM, STREAM[1:])):
        source = beam_hbm.at[pl.ds(begin, end - begin)]
        target = beam.at[pl.ds(begin - HELD, end - begin)]
        copies[begin] = pltpu.make_async_copy(source, target, sems.at[i])
        copies[begin].start()

    at = lax.broadcasted_iota(I32, (L, OWNERS), 0)
    for q in range(ROWCAP):
        wanted = wanted_ref[q : q + 1, :]
        pick[:, q * OWNERS : (q + 1) * OWNERS] = ones_where(at == wanted)

    total = sums_ref[pl.ds(0, SLOTS * INNER), :]
    for z in range(1, OUTER):
        total = total + sums_ref[pl.ds(z * SLOTS * INNER, SLOTS * INNER), :]
    low = low_lanes((8, LANES))
    with_re, with_im = [], []
    for j in range(INNER // 2):
        tile = total[8 * j : 8 * j + 8]
        rolled = pltpu.roll(tile, HALF, 1)
        re = jnp.where(low, tile, pltpu.roll(rolled, 4, 0))[:4]
        im = jnp.where(low, rolled, pltpu.roll(tile, 4, 0))[:4]
        with_re.append(jnp.concatenate([re, im], axis=0))
        with_im.append(jnp.concatenate([im, -re], axis=0))
    weights = jnp.concatenate(with_re + with_im, axis=1).astype(BF16)
    depth = weights.shape[1] // PARTS

    def product(i):
        if i < HELD:
            block = held_ref[i]
        else:
            if i in copies:
                copies[i].wait()
            block = beam[i - HELD]
        part = i % PARTS * depth
        return jnp.dot(weights[:, part : part + depth], block, preferred_element_type=F32)

    alm = [None] * 8
    for k in range(SLOTS):
        both = sum(product(k * PARTS + part) for part in range(PARTS))
        at = k // 2 * 4 + k % 2
        alm[at] = both[k : k + 1]
        alm[at + 2] = both[4 + k : 5 + k]
    alm = jnp.where(keep_ref[...] > 0.0, jnp.concatenate(alm, axis=0), 0.0)
    alm = jnp.concatenate(split(alm), axis=0)

    wide = jnp.dot(alm, pick[...], preferred_element_type=F32)
    wide = wide[:8] + wide[8:]
    first = core_ref[:4] == 0
    for q in range(ROWCAP):
        block = wide[:, q * OWNERS : (q + 1) * OWNERS]
        rows_at = pl.ds(q, 4, stride=ROWCAP)
        own_ref[rows_at, :] = jnp.where(first, block[:4], block[4:])
        other_ref[rows_at, :] = jnp.where(first, block[4:], block[:4])


def finish_kernel(parts_ref, out_ref):
    starts = [8 * (i ^ FIRST_LAST // 8) for i in range(OWNERS // 8)]
    tiles = [parts_ref[start : start + 8, :] for start in starts]
    out_ref[...] = lane_xor(jnp.concatenate(tiles, axis=0).T, FIRST_LAST % 8)


def exchange(array, first, size):
    groups = [
        [base + (rank ^ first) for rank in range(size)] for base in range(0, OWNERS, size)
    ]
    return lax.all_to_all(array, "ma", 0, 0, axis_index_groups=groups, tiled=True)


def call(kernel, out_shape, in_specs, scratch_shapes=(), scoped=8):
    return pl.pallas_call(
        kernel,
        out_shape=out_shape,
        in_specs=in_specs,
        out_specs=jax.tree.map(
            lambda a: pl.BlockSpec(memory_space=getattr(a, "memory_space", pltpu.VMEM)), out_shape
        ),
        scratch_shapes=scratch_shapes,
        compiler_params=pltpu.CompilerParams(vmem_limit_bytes=scoped * 1024 * 1024),
    )


def in_hbm(array):
    return pltpu.with_memory_space_constraint(array, pltpu.HBM)


def in_vmem(array):
    return pltpu.with_memory_space_constraint(array, pltpu.VMEM)


def body(vis, counts, m_order, beam, row_counts):
    place = lax.axis_index("ma")
    share = vis.shape[1]
    blocks = vis.shape[2] // LANES
    table = transform_table()
    dma = pltpu.SemaphoreType.DMA

    packed = call(
        pack_kernel,
        pltpu.HBM((INNER, share, LANES), F32),
        [HBM, HBM],
        [
            pltpu.VMEM(vis.shape, F32),
            pltpu.VMEM((blocks, LANES), I32),
            pltpu.VMEM((INNER, share, LANES), F32),
            dma((2,)),
            dma((2,)),
        ],
    )(in_hbm(vis), in_hbm(counts.reshape(blocks, LANES)))
    gathered = exchange(packed, FIRST_INNER, INNER)

    beam = in_hbm(beam.reshape(SLOTS * PARTS, -1, L))
    high, low, *held = call(
        tables_kernel,
        (
            pltpu.VMEM(table.shape, BF16),
            pltpu.VMEM(table.shape, BF16),
            pltpu.VMEM((HELD, *beam.shape[1:]), BF16),
            pltpu.VMEM((ROWCAP, OWNERS), I32),
            pltpu.VMEM((8, L), F32),
            pltpu.VMEM((8, LANES), I32),
        ),
        [SMEM] + [HBM] * 5,
        [
            pltpu.VMEM(table.shape, F32),
            pltpu.VMEM(table.shape, BF16),
            pltpu.VMEM(table.shape, BF16),
            pltpu.VMEM((L, L), BF16),
            pltpu.VMEM((8, LANES), I32),
            pltpu.SMEM((L,), I32),
            pltpu.VMEM((1, OWNERS), I32),
            dma((L // LANES + 4,)),
        ],
        scoped=16,
    )(
        jnp.stack([place, lax.axis_index("bl")]).astype(I32),
        in_hbm(jnp.asarray(table)),
        in_hbm(m_order.reshape(L // LANES, LANES)),
        in_hbm(m_order),
        in_hbm(row_counts.reshape(1, OWNERS)),
        beam,
    )
    modes = call(transform_kernel, pltpu.VMEM((L, LANES), F32), [VMEM] * 3)(
        gathered.reshape(SPAN, LANES), in_vmem(high), in_vmem(low)
    )
    sums = exchange(modes.reshape(OWNERS, SLOTS, LANES), FIRST, OWNERS)

    half = pltpu.VMEM((4 * ROWCAP, OWNERS), F32)
    streamed = SLOTS * PARTS - HELD
    own, other = call(
        project_kernel,
        (half, half),
        [VMEM] * 5 + [HBM],
        [
            pltpu.VMEM((streamed, *beam.shape[1:]), BF16),
            pltpu.VMEM((L, ROWCAP * OWNERS), BF16),
            dma((len(STREAM) - 1,)),
        ],
        scoped=24,
    )(
        sums.reshape(OWNERS * SLOTS, LANES),
        *map(in_vmem, held),
        beam,
    )
    picked = own + lax.ppermute(other, "bl", [(0, 1), (1, 0)])
    received = exchange(picked.T, FIRST_LAST, OWNERS)
    out = call(finish_kernel, jax.ShapeDtypeStruct((4 * ROWCAP, OWNERS), F32), [VMEM])(received)
    return out.reshape(2, 2, ROWCAP, OWNERS).transpose(0, 3, 1, 2)


def solution(mesh):
    placed = (P(None, "ma", "bl"), P("bl"), P(), P("ma", None, "bl", None), P())
    return jax.shard_map(
        body, mesh=mesh, in_specs=placed, out_specs=P(None, None, "bl", "ma"), check_vma=False
    )
```

```python
import numpy as np
import jax
import jax.numpy as jnp
from jax import lax
from jax.experimental import pallas as pl
from jax.experimental.pallas import tpu as pltpu
from jax.sharding import PartitionSpec as P

L = 512
TIMES = 4096
OUTER = 8
INNER = 16
SPAN = TIMES // OUTER
OWNERS = OUTER * INNER
SLOTS = 4
ROWCAP = 8
LANES = 128
HALF = 64
PARTS = 4
HELD = 2
STREAM = (HELD, 10, 14, SLOTS * PARTS)
FIRST_INNER = 10
FIRST_OUTER = 5
FIRST_PLANE = 6
FIRST = FIRST_OUTER * INNER + FIRST_INNER
FIRST_LAST = 74

F32 = jnp.float32
BF16 = jnp.bfloat16
I32 = jnp.int32
VMEM = pl.BlockSpec(memory_space=pltpu.VMEM)
SMEM = pl.BlockSpec(memory_space=pltpu.SMEM)
HBM = pl.BlockSpec(memory_space=pltpu.HBM)


def transform_table():
    times = np.arange(SPAN).reshape(INNER, -1)[np.arange(INNER) ^ FIRST_PLANE]
    turns = np.outer(np.arange(L), times) % TIMES
    phase = 2.0 * np.pi / TIMES * turns
    table = np.concatenate([np.cos(phase), np.sin(phase)], axis=1) / np.sqrt(TIMES)
    return table.astype(np.float32)


def low_lanes(shape):
    return lax.broadcasted_iota(I32, shape, 1) < HALF


def quarter_turn(pair):
    turned = pltpu.roll(pair, HALF, 1)
    return jnp.where(low_lanes(pair.shape), turned, -turned)


def split(array):
    high = array.astype(BF16)
    return high, (array - high.astype(F32)).astype(BF16)


def lane_xor(array, mask):
    lane = lax.broadcasted_iota(I32, array.shape, 1)
    for bit in range(7):
        step = 1 << bit
        if mask & step:
            up = pltpu.roll(array, LANES - step, 1)
            array = jnp.where(lane & step == 0, up, pltpu.roll(array, step, 1))
    return array


def ones_where(condition):
    return jnp.where(condition, 1.0, 0.0).astype(BF16)


def pack_kernel(vis_ref, counts_ref, out_ref, vis, counts, packed, in_sems, out_sems):
    copies = [
        pltpu.make_async_copy(vis_ref, vis, in_sems.at[0]),
        pltpu.make_async_copy(counts_ref, counts, in_sems.at[1]),
    ]
    for copy in copies:
        copy.start()
    for copy in copies:
        copy.wait()

    def store(i):
        part = pl.ds(i * INNER // 2, INNER // 2)
        return pltpu.make_async_copy(packed.at[part], out_ref.at[part], out_sems.at[i])

    blocks = vis.shape[2] // LANES
    low = low_lanes((vis.shape[1], LANES))
    for j in range(blocks):
        lanes = slice(j * LANES, (j + 1) * LANES)
        scale = counts[j : j + 1, :].astype(F32) * (1.0 / 256.0)
        re = vis[0, :, lanes] * scale
        im = vis[1, :, lanes] * scale
        packed[2 * j] = jnp.where(low, re, pltpu.roll(im, HALF, 1))
        packed[2 * j + 1] = jnp.where(low, pltpu.roll(re, HALF, 1), im)
        if j % (blocks // 2) == blocks // 2 - 1:
            store(2 * j // blocks).start()
    for i in range(2):
        store(i).wait()


def tables_kernel(
    place_ref,
    table_hbm,
    lanes_hbm,
    order_hbm,
    rows_hbm,
    beam_hbm,
    high_ref,
    low_ref,
    held_ref,
    wanted_ref,
    keep_ref,
    core_ref,
    table,
    high,
    low,
    pick,
    lanes,
    order,
    rows,
    sems,
):
    lanes_copy = pltpu.make_async_copy(lanes_hbm, lanes.at[pl.ds(0, L // LANES)], sems.at[0])
    order_copy = pltpu.make_async_copy(order_hbm, order, sems.at[1])
    rows_copy = pltpu.make_async_copy(rows_hbm, rows, sems.at[2])
    held_copy = pltpu.make_async_copy(beam_hbm.at[pl.ds(0, HELD)], held_ref, sems.at[3])
    lanes_copy.start()
    order_copy.start()
    rows_copy.start()

    def fetch(i):
        part = pl.ds(i * LANES, LANES)
        return pltpu.make_async_copy(table_hbm.at[part], table.at[part], sems.at[i + 4])

    for i in range(L // LANES):
        fetch(i).start()
    held_copy.start()
    eighths = lax.broadcasted_iota(I32, (8, LANES), 0) * (place_ref[0] // INNER) % 8
    angle = eighths.astype(F32) * (2.0 * np.pi / 8)
    along = jnp.cos(angle)[None, :, :1]
    across = jnp.sin(angle)[None, :, :1]

    lanes_copy.wait()
    columns = lane_xor(lanes[...], SLOTS * FIRST % LANES).T
    modes = lax.broadcasted_iota(I32, (LANES, L), 1)
    for i in range(L // LANES):
        block = i ^ SLOTS * FIRST // LANES
        pick[i * LANES : (i + 1) * LANES, :] = ones_where(modes == columns[:, block : block + 1])

    core_ref[...] = jnp.broadcast_to(place_ref[1], (8, LANES))
    order_copy.wait()
    ells = lax.broadcasted_iota(I32, (1, L), 1)
    for k in range(SLOTS):
        keep = jnp.where(ells >= order[place_ref[0] * SLOTS + k], 1.0, 0.0)
        at = k // 2 * 4 + k % 2
        keep_ref[at : at + 1, :] = keep
        keep_ref[at + 2 : at + 3, :] = keep

    rows_copy.wait()
    counts = jnp.broadcast_to(rows[...], (ROWCAP, OWNERS)).astype(F32).astype(BF16)
    other = lax.broadcasted_iota(I32, (OWNERS, OWNERS), 0)
    owner = lax.broadcasted_iota(I32, (OWNERS, OWNERS), 1) ^ FIRST_LAST
    starts = jnp.dot(counts, ones_where(other < owner), preferred_element_type=F32)
    counts = jnp.dot(counts, ones_where(other == owner), preferred_element_type=F32)
    counts = counts.astype(I32)
    within = lax.broadcasted_iota(I32, (ROWCAP, OWNERS), 0)
    wanted_ref[...] = jnp.where(within < counts, starts.astype(I32) + within, -1)

    for i in range(L // LANES):
        fetch(i).wait()
        part = slice(i * LANES, (i + 1) * LANES)
        cosine = table[part, :SPAN].reshape(LANES // 8, 8, SPAN)
        sine = table[part, SPAN:].reshape(LANES // 8, 8, SPAN)
        turned = [cosine * along - sine * across, sine * along + cosine * across]
        turned = jnp.concatenate([half.reshape(LANES, SPAN) for half in turned], axis=1)
        high[part, :], low[part, :] = split(turned)
    for i in range(L // LANES):
        part = slice(i * LANES, (i + 1) * LANES)
        for source, out_ref in ((high, high_ref), (low, low_ref)):
            picked = jnp.dot(pick[part, :], source[...], preferred_element_type=F32)
            out_ref[part, :] = picked.astype(BF16)
    held_copy.wait()


def transform_kernel(x_ref, high_ref, low_ref, out_ref):
    x = x_ref[...]
    high, low = split(jnp.concatenate([x, quarter_turn(x)], axis=0))
    both = jnp.concatenate([high, low], axis=1)
    wide = jnp.dot(high_ref[...], both, preferred_element_type=F32)
    slots = jnp.dot(low_ref[...], high, preferred_element_type=F32)
    out_ref[...] = slots + wide[:, :LANES] + wide[:, LANES:]


def project_kernel(
    sums_ref,
    held_ref,
    wanted_ref,
    keep_ref,
    core_ref,
    beam_hbm,
    own_ref,
    other_ref,
    beam,
    pick,
    sems,
):
    copies = {}
    for i, (begin, end) in enumerate(zip(STREAM, STREAM[1:])):
        source = beam_hbm.at[pl.ds(begin, end - begin)]
        target = beam.at[pl.ds(begin - HELD, end - begin)]
        copies[begin] = pltpu.make_async_copy(source, target, sems.at[i])
        copies[begin].start()

    at = lax.broadcasted_iota(I32, (L, OWNERS), 0)
    for q in range(ROWCAP):
        wanted = wanted_ref[q : q + 1, :]
        pick[:, q * OWNERS : (q + 1) * OWNERS] = ones_where(at == wanted)

    total = sums_ref[pl.ds(0, SLOTS * INNER), :]
    for z in range(1, OUTER):
        total = total + sums_ref[pl.ds(z * SLOTS * INNER, SLOTS * INNER), :]
    low = low_lanes((8, LANES))
    with_re, with_im = [], []
    for j in range(INNER // 2):
        at = 8 * (j ^ (FIRST_PLANE ^ FIRST_INNER) // 2)
        tile = total[at : at + 8]
        rolled = pltpu.roll(tile, HALF, 1)
        re = jnp.where(low, tile, pltpu.roll(rolled, 4, 0))[:4]
        im = jnp.where(low, rolled, pltpu.roll(tile, 4, 0))[:4]
        with_re.append(jnp.concatenate([re, im], axis=0))
        with_im.append(jnp.concatenate([im, -re], axis=0))
    weights = jnp.concatenate(with_re + with_im, axis=1).astype(BF16)
    depth = weights.shape[1] // PARTS

    def product(i):
        if i < HELD:
            block = held_ref[i]
        else:
            if i in copies:
                copies[i].wait()
            block = beam[i - HELD]
        part = i % PARTS * depth
        return jnp.dot(weights[:, part : part + depth], block, preferred_element_type=F32)

    alm = [None] * 8
    for k in range(SLOTS):
        both = sum(product(k * PARTS + part) for part in range(PARTS))
        at = k // 2 * 4 + k % 2
        alm[at] = both[k : k + 1]
        alm[at + 2] = both[4 + k : 5 + k]
    alm = jnp.where(keep_ref[...] > 0.0, jnp.concatenate(alm, axis=0), 0.0)
    alm = jnp.concatenate(split(alm), axis=0)

    wide = jnp.dot(alm, pick[...], preferred_element_type=F32)
    wide = wide[:8] + wide[8:]
    first = core_ref[:4] == 0
    for q in range(ROWCAP):
        block = wide[:, q * OWNERS : (q + 1) * OWNERS]
        rows_at = pl.ds(q, 4, stride=ROWCAP)
        own_ref[rows_at, :] = jnp.where(first, block[:4], block[4:])
        other_ref[rows_at, :] = jnp.where(first, block[4:], block[:4])


def finish_kernel(parts_ref, out_ref):
    starts = [8 * (i ^ FIRST_LAST // 8) for i in range(OWNERS // 8)]
    tiles = [parts_ref[start : start + 8, :] for start in starts]
    out_ref[...] = lane_xor(jnp.concatenate(tiles, axis=0).T, FIRST_LAST % 8)


def exchange(array, first, size):
    groups = [
        [base + (rank ^ first) for rank in range(size)] for base in range(0, OWNERS, size)
    ]
    return lax.all_to_all(array, "ma", 0, 0, axis_index_groups=groups, tiled=True)


def call(kernel, out_shape, in_specs, scratch_shapes=(), scoped=8):
    return pl.pallas_call(
        kernel,
        out_shape=out_shape,
        in_specs=in_specs,
        out_specs=jax.tree.map(
            lambda a: pl.BlockSpec(memory_space=getattr(a, "memory_space", pltpu.VMEM)), out_shape
        ),
        scratch_shapes=scratch_shapes,
        compiler_params=pltpu.CompilerParams(vmem_limit_bytes=scoped * 1024 * 1024),
    )


def in_hbm(array):
    return pltpu.with_memory_space_constraint(array, pltpu.HBM)


def in_vmem(array):
    return pltpu.with_memory_space_constraint(array, pltpu.VMEM)


def body(vis, counts, m_order, beam, row_counts):
    place = lax.axis_index("ma")
    share = vis.shape[1]
    blocks = vis.shape[2] // LANES
    table = transform_table()
    dma = pltpu.SemaphoreType.DMA

    packed = call(
        pack_kernel,
        pltpu.HBM((INNER, share, LANES), F32),
        [HBM, HBM],
        [
            pltpu.VMEM(vis.shape, F32),
            pltpu.VMEM((blocks, LANES), I32),
            pltpu.VMEM((INNER, share, LANES), F32),
            dma((2,)),
            dma((2,)),
        ],
    )(in_hbm(vis), in_hbm(counts.reshape(blocks, LANES)))
    gathered = exchange(packed, FIRST_PLANE, INNER)

    beam = in_hbm(beam.reshape(SLOTS * PARTS, -1, L))
    high, low, *held = call(
        tables_kernel,
        (
            pltpu.VMEM(table.shape, BF16),
            pltpu.VMEM(table.shape, BF16),
            pltpu.VMEM((HELD, *beam.shape[1:]), BF16),
            pltpu.VMEM((ROWCAP, OWNERS), I32),
            pltpu.VMEM((8, L), F32),
            pltpu.VMEM((8, LANES), I32),
        ),
        [SMEM] + [HBM] * 5,
        [
            pltpu.VMEM(table.shape, F32),
            pltpu.VMEM(table.shape, BF16),
            pltpu.VMEM(table.shape, BF16),
            pltpu.VMEM((L, L), BF16),
            pltpu.VMEM((8, LANES), I32),
            pltpu.SMEM((L,), I32),
            pltpu.VMEM((1, OWNERS), I32),
            dma((L // LANES + 4,)),
        ],
        scoped=16,
    )(
        jnp.stack([place, lax.axis_index("bl")]).astype(I32),
        in_hbm(jnp.asarray(table)),
        in_hbm(m_order.reshape(L // LANES, LANES)),
        in_hbm(m_order),
        in_hbm(row_counts.reshape(1, OWNERS)),
        beam,
    )
    modes = call(transform_kernel, pltpu.VMEM((L, LANES), F32), [VMEM] * 3)(
        gathered.reshape(SPAN, LANES), in_vmem(high), in_vmem(low)
    )
    sums = exchange(modes.reshape(OWNERS, SLOTS, LANES), FIRST, OWNERS)

    half = pltpu.VMEM((4 * ROWCAP, OWNERS), F32)
    streamed = SLOTS * PARTS - HELD
    own, other = call(
        project_kernel,
        (half, half),
        [VMEM] * 5 + [HBM],
        [
            pltpu.VMEM((streamed, *beam.shape[1:]), BF16),
            pltpu.VMEM((L, ROWCAP * OWNERS), BF16),
            dma((len(STREAM) - 1,)),
        ],
        scoped=24,
    )(
        sums.reshape(OWNERS * SLOTS, LANES),
        *map(in_vmem, held),
        beam,
    )
    picked = own + lax.ppermute(other, "bl", [(0, 1), (1, 0)])
    received = exchange(picked.T, FIRST_LAST, OWNERS)
    out = call(finish_kernel, jax.ShapeDtypeStruct((4 * ROWCAP, OWNERS), F32), [VMEM])(received)
    return out.reshape(2, 2, ROWCAP, OWNERS).transpose(0, 3, 1, 2)


def solution(mesh):
    placed = (P(None, "ma", "bl"), P("bl"), P(), P("ma", None, "bl", None), P())
    return jax.shard_map(
        body, mesh=mesh, in_specs=placed, out_specs=P(None, None, "bl", "ma"), check_vma=False
    )
```

```python
import numpy as np
import jax
import jax.numpy as jnp
from jax import lax
from jax.experimental import pallas as pl
from jax.experimental.pallas import tpu as pltpu
from jax.sharding import PartitionSpec as P

L = 512
TIMES = 4096
OUTER = 8
INNER = 16
SPAN = TIMES // OUTER
OWNERS = OUTER * INNER
SLOTS = 4
ROWCAP = 8
LANES = 128
HALF = 64
PARTS = 4
HELD = 2
MORE = 4
STREAM = (HELD + MORE, 10, 14, SLOTS * PARTS)
FIRST_INNER = 10
FIRST_OUTER = 5
FIRST_PLANE = 6
FIRST = FIRST_OUTER * INNER + FIRST_INNER
FIRST_LAST = 74

F32 = jnp.float32
BF16 = jnp.bfloat16
I32 = jnp.int32
VMEM = pl.BlockSpec(memory_space=pltpu.VMEM)
SMEM = pl.BlockSpec(memory_space=pltpu.SMEM)
HBM = pl.BlockSpec(memory_space=pltpu.HBM)


def transform_table():
    times = np.arange(SPAN).reshape(INNER, -1)[np.arange(INNER) ^ FIRST_PLANE]
    turns = np.outer(np.arange(L), times) % TIMES
    phase = 2.0 * np.pi / TIMES * turns
    table = np.concatenate([np.cos(phase), np.sin(phase)], axis=1) / np.sqrt(TIMES)
    return table.astype(np.float32)


def low_lanes(shape):
    return lax.broadcasted_iota(I32, shape, 1) < HALF


def quarter_turn(pair):
    turned = pltpu.roll(pair, HALF, 1)
    return jnp.where(low_lanes(pair.shape), turned, -turned)


def split(array):
    high = array.astype(BF16)
    return high, (array - high.astype(F32)).astype(BF16)


def lane_xor(array, mask):
    lane = lax.broadcasted_iota(I32, array.shape, 1)
    for bit in range(7):
        step = 1 << bit
        if mask & step:
            up = pltpu.roll(array, LANES - step, 1)
            array = jnp.where(lane & step == 0, up, pltpu.roll(array, step, 1))
    return array


def ones_where(condition):
    return jnp.where(condition, 1.0, 0.0).astype(BF16)


def pack_kernel(vis_ref, counts_ref, out_ref, vis, counts, packed, in_sems, out_sems):
    copies = [
        pltpu.make_async_copy(vis_ref, vis, in_sems.at[0]),
        pltpu.make_async_copy(counts_ref, counts, in_sems.at[1]),
    ]
    for copy in copies:
        copy.start()
    for copy in copies:
        copy.wait()

    def store(i):
        part = pl.ds(i * INNER // 2, INNER // 2)
        return pltpu.make_async_copy(packed.at[part], out_ref.at[part], out_sems.at[i])

    blocks = vis.shape[2] // LANES
    low = low_lanes((vis.shape[1], LANES))
    for j in range(blocks):
        lanes = slice(j * LANES, (j + 1) * LANES)
        scale = counts[j : j + 1, :].astype(F32) * (1.0 / 256.0)
        re = vis[0, :, lanes] * scale
        im = vis[1, :, lanes] * scale
        packed[2 * j] = jnp.where(low, re, pltpu.roll(im, HALF, 1))
        packed[2 * j + 1] = jnp.where(low, pltpu.roll(re, HALF, 1), im)
        if j % (blocks // 2) == blocks // 2 - 1:
            store(2 * j // blocks).start()
    for i in range(2):
        store(i).wait()


def tables_kernel(
    place_ref,
    table_hbm,
    lanes_hbm,
    order_hbm,
    rows_hbm,
    beam_hbm,
    high_ref,
    low_ref,
    held_ref,
    wanted_ref,
    keep_ref,
    core_ref,
    table,
    high,
    low,
    pick,
    lanes,
    order,
    rows,
    sems,
):
    lanes_copy = pltpu.make_async_copy(lanes_hbm, lanes.at[pl.ds(0, L // LANES)], sems.at[0])
    order_copy = pltpu.make_async_copy(order_hbm, order, sems.at[1])
    rows_copy = pltpu.make_async_copy(rows_hbm, rows, sems.at[2])
    held_copy = pltpu.make_async_copy(beam_hbm.at[pl.ds(0, HELD)], held_ref, sems.at[3])
    lanes_copy.start()
    order_copy.start()
    rows_copy.start()

    def fetch(i):
        part = pl.ds(i * LANES, LANES)
        return pltpu.make_async_copy(table_hbm.at[part], table.at[part], sems.at[i + 4])

    for i in range(L // LANES):
        fetch(i).start()
    held_copy.start()
    eighths = lax.broadcasted_iota(I32, (8, LANES), 0) * (place_ref[0] // INNER) % 8
    angle = eighths.astype(F32) * (2.0 * np.pi / 8)
    along = jnp.cos(angle)[None, :, :1]
    across = jnp.sin(angle)[None, :, :1]

    lanes_copy.wait()
    columns = lane_xor(lanes[...], SLOTS * FIRST % LANES).T
    modes = lax.broadcasted_iota(I32, (LANES, L), 1)
    for i in range(L // LANES):
        block = i ^ SLOTS * FIRST // LANES
        pick[i * LANES : (i + 1) * LANES, :] = ones_where(modes == columns[:, block : block + 1])

    core_ref[...] = jnp.broadcast_to(place_ref[1], (8, LANES))
    order_copy.wait()
    ells = lax.broadcasted_iota(I32, (1, L), 1)
    for k in range(SLOTS):
        keep = jnp.where(ells >= order[place_ref[0] * SLOTS + k], 1.0, 0.0)
        at = k // 2 * 4 + k % 2
        keep_ref[at : at + 1, :] = keep
        keep_ref[at + 2 : at + 3, :] = keep

    rows_copy.wait()
    counts = jnp.broadcast_to(rows[...], (ROWCAP, OWNERS)).astype(F32).astype(BF16)
    other = lax.broadcasted_iota(I32, (OWNERS, OWNERS), 0)
    owner = lax.broadcasted_iota(I32, (OWNERS, OWNERS), 1) ^ FIRST_LAST
    starts = jnp.dot(counts, ones_where(other < owner), preferred_element_type=F32)
    counts = jnp.dot(counts, ones_where(other == owner), preferred_element_type=F32)
    counts = counts.astype(I32)
    within = lax.broadcasted_iota(I32, (ROWCAP, OWNERS), 0)
    wanted_ref[...] = jnp.where(within < counts, starts.astype(I32) + within, -1)

    for i in range(L // LANES):
        fetch(i).wait()
        part = slice(i * LANES, (i + 1) * LANES)
        cosine = table[part, :SPAN].reshape(LANES // 8, 8, SPAN)
        sine = table[part, SPAN:].reshape(LANES // 8, 8, SPAN)
        turned = [cosine * along - sine * across, sine * along + cosine * across]
        turned = jnp.concatenate([half.reshape(LANES, SPAN) for half in turned], axis=1)
        high[part, :], low[part, :] = split(turned)
    for i in range(L // LANES):
        part = slice(i * LANES, (i + 1) * LANES)
        for source, out_ref in ((high, high_ref), (low, low_ref)):
            picked = jnp.dot(pick[part, :], source[...], preferred_element_type=F32)
            out_ref[part, :] = picked.astype(BF16)
    held_copy.wait()


def transform_kernel(
    x_ref, high_ref, low_ref, core_ref, beam_hbm, out_ref, more_ref, sem
):
    first = core_ref[0, 0] == 0
    copy = pltpu.make_async_copy(beam_hbm.at[pl.ds(HELD, MORE)], more_ref, sem)
    pl.when(first)(copy.start)
    x = x_ref[...]
    high, low = split(jnp.concatenate([x, quarter_turn(x)], axis=0))
    both = jnp.concatenate([high, low], axis=1)
    wide = jnp.dot(high_ref[...], both, preferred_element_type=F32)
    slots = jnp.dot(low_ref[...], high, preferred_element_type=F32)
    out_ref[...] = slots + wide[:, :LANES] + wide[:, LANES:]
    pl.when(first)(copy.wait)


def project_kernel(
    sums_ref,
    held_ref,
    wanted_ref,
    keep_ref,
    core_ref,
    more_ref,
    beam_hbm,
    own_ref,
    other_ref,
    beam,
    pick,
    more,
    sems,
    more_sem,
):
    first = core_ref[0, 0] == 0
    more_copy = pltpu.make_async_copy(
        beam_hbm.at[pl.ds(HELD, MORE)], beam.at[pl.ds(0, MORE)], more_sem
    )
    pl.when(jnp.logical_not(first))(more_copy.start)
    copies = {}
    for i, (begin, end) in enumerate(zip(STREAM, STREAM[1:])):
        source = beam_hbm.at[pl.ds(begin, end - begin)]
        target = beam.at[pl.ds(begin - HELD, end - begin)]
        copies[begin] = pltpu.make_async_copy(source, target, sems.at[i])
        copies[begin].start()

    at = lax.broadcasted_iota(I32, (L, OWNERS), 0)
    for q in range(ROWCAP):
        wanted = wanted_ref[q : q + 1, :]
        pick[:, q * OWNERS : (q + 1) * OWNERS] = ones_where(at == wanted)

    total = sums_ref[pl.ds(0, SLOTS * INNER), :]
    for z in range(1, OUTER):
        total = total + sums_ref[pl.ds(z * SLOTS * INNER, SLOTS * INNER), :]
    low = low_lanes((8, LANES))
    with_re, with_im = [], []
    for j in range(INNER // 2):
        at = 8 * (j ^ (FIRST_PLANE ^ FIRST_INNER) // 2)
        tile = total[at : at + 8]
        rolled = pltpu.roll(tile, HALF, 1)
        re = jnp.where(low, tile, pltpu.roll(rolled, 4, 0))[:4]
        im = jnp.where(low, rolled, pltpu.roll(tile, 4, 0))[:4]
        with_re.append(jnp.concatenate([re, im], axis=0))
        with_im.append(jnp.concatenate([im, -re], axis=0))
    weights = jnp.concatenate(with_re + with_im, axis=1).astype(BF16)
    depth = weights.shape[1] // PARTS

    def product(i, block):
        part = i % PARTS * depth
        return jnp.dot(weights[:, part : part + depth], block, preferred_element_type=F32)

    def add_more(blocks):
        for k in range(2):
            indices = [i for i in range(HELD, HELD + MORE) if i // PARTS == k]
            more[k] = sum(product(i, blocks[i - HELD]) for i in indices)

    @pl.when(first)
    def _():
        add_more(more_ref)

    @pl.when(jnp.logical_not(first))
    def _():
        more_copy.wait()
        add_more(beam)

    alm = [None] * 8
    for k in range(SLOTS):
        both = more[k] if k < 2 else jnp.zeros((8, L), F32)
        for i in range(k * PARTS, (k + 1) * PARTS):
            if i in copies:
                copies[i].wait()
            if i < HELD:
                both = both + product(i, held_ref[i])
            elif i >= HELD + MORE:
                both = both + product(i, beam[i - HELD])
        at = k // 2 * 4 + k % 2
        alm[at] = both[k : k + 1]
        alm[at + 2] = both[4 + k : 5 + k]
    alm = jnp.where(keep_ref[...] > 0.0, jnp.concatenate(alm, axis=0), 0.0)
    alm = jnp.concatenate(split(alm), axis=0)

    wide = jnp.dot(alm, pick[...], preferred_element_type=F32)
    wide = wide[:8] + wide[8:]
    first = core_ref[:4] == 0
    for q in range(ROWCAP):
        block = wide[:, q * OWNERS : (q + 1) * OWNERS]
        rows_at = pl.ds(q, 4, stride=ROWCAP)
        own_ref[rows_at, :] = jnp.where(first, block[:4], block[4:])
        other_ref[rows_at, :] = jnp.where(first, block[4:], block[:4])


def finish_kernel(parts_ref, out_ref):
    starts = [8 * (i ^ FIRST_LAST // 8) for i in range(OWNERS // 8)]
    tiles = [parts_ref[start : start + 8, :] for start in starts]
    out_ref[...] = lane_xor(jnp.concatenate(tiles, axis=0).T, FIRST_LAST % 8)


def exchange(array, first, size):
    groups = [
        [base + (rank ^ first) for rank in range(size)] for base in range(0, OWNERS, size)
    ]
    return lax.all_to_all(array, "ma", 0, 0, axis_index_groups=groups, tiled=True)


def call(kernel, out_shape, in_specs, scratch_shapes=(), scoped=8):
    return pl.pallas_call(
        kernel,
        out_shape=out_shape,
        in_specs=in_specs,
        out_specs=jax.tree.map(
            lambda a: pl.BlockSpec(memory_space=getattr(a, "memory_space", pltpu.VMEM)), out_shape
        ),
        scratch_shapes=scratch_shapes,
        compiler_params=pltpu.CompilerParams(vmem_limit_bytes=scoped * 1024 * 1024),
    )


def in_hbm(array):
    return pltpu.with_memory_space_constraint(array, pltpu.HBM)


def in_vmem(array):
    return pltpu.with_memory_space_constraint(array, pltpu.VMEM)


def body(vis, counts, m_order, beam, row_counts):
    place = lax.axis_index("ma")
    share = vis.shape[1]
    blocks = vis.shape[2] // LANES
    table = transform_table()
    dma = pltpu.SemaphoreType.DMA

    packed = call(
        pack_kernel,
        pltpu.HBM((INNER, share, LANES), F32),
        [HBM, HBM],
        [
            pltpu.VMEM(vis.shape, F32),
            pltpu.VMEM((blocks, LANES), I32),
            pltpu.VMEM((INNER, share, LANES), F32),
            dma((2,)),
            dma((2,)),
        ],
    )(in_hbm(vis), in_hbm(counts.reshape(blocks, LANES)))
    gathered = exchange(packed, FIRST_PLANE, INNER)

    beam = in_hbm(beam.reshape(SLOTS * PARTS, -1, L))
    high, low, *held = call(
        tables_kernel,
        (
            pltpu.VMEM(table.shape, BF16),
            pltpu.VMEM(table.shape, BF16),
            pltpu.VMEM((HELD, *beam.shape[1:]), BF16),
            pltpu.VMEM((ROWCAP, OWNERS), I32),
            pltpu.VMEM((8, L), F32),
            pltpu.VMEM((8, LANES), I32),
        ),
        [SMEM] + [HBM] * 5,
        [
            pltpu.VMEM(table.shape, F32),
            pltpu.VMEM(table.shape, BF16),
            pltpu.VMEM(table.shape, BF16),
            pltpu.VMEM((L, L), BF16),
            pltpu.VMEM((8, LANES), I32),
            pltpu.SMEM((L,), I32),
            pltpu.VMEM((1, OWNERS), I32),
            dma((L // LANES + 4,)),
        ],
        scoped=16,
    )(
        jnp.stack([place, lax.axis_index("bl")]).astype(I32),
        in_hbm(jnp.asarray(table)),
        in_hbm(m_order.reshape(L // LANES, LANES)),
        in_hbm(m_order),
        in_hbm(row_counts.reshape(1, OWNERS)),
        beam,
    )
    modes, more = call(
        transform_kernel,
        (pltpu.VMEM((L, LANES), F32), pltpu.VMEM((MORE, *beam.shape[1:]), BF16)),
        [VMEM] * 4 + [HBM],
        [dma(())],
    )(gathered.reshape(SPAN, LANES), in_vmem(high), in_vmem(low), in_vmem(held[-1]), beam)
    sums = exchange(modes.reshape(OWNERS, SLOTS, LANES), FIRST, OWNERS)

    half = pltpu.VMEM((4 * ROWCAP, OWNERS), F32)
    streamed = SLOTS * PARTS - HELD
    own, other = call(
        project_kernel,
        (half, half),
        [VMEM] * 6 + [HBM],
        [
            pltpu.VMEM((streamed, *beam.shape[1:]), BF16),
            pltpu.VMEM((L, ROWCAP * OWNERS), BF16),
            pltpu.VMEM((2, 8, L), F32),
            dma((len(STREAM) - 1,)),
            dma(()),
        ],
        scoped=24,
    )(
        sums.reshape(OWNERS * SLOTS, LANES),
        *map(in_vmem, held),
        in_vmem(more),
        beam,
    )
    picked = own + lax.ppermute(other, "bl", [(0, 1), (1, 0)])
    received = exchange(picked.T, FIRST_LAST, OWNERS)
    out = call(finish_kernel, jax.ShapeDtypeStruct((4 * ROWCAP, OWNERS), F32), [VMEM])(received)
    return out.reshape(2, 2, ROWCAP, OWNERS).transpose(0, 3, 1, 2)


def solution(mesh):
    placed = (P(None, "ma", "bl"), P("bl"), P(), P("ma", None, "bl", None), P())
    return jax.shard_map(
        body, mesh=mesh, in_specs=placed, out_specs=P(None, None, "bl", "ma"), check_vma=False
    )
```
